256 devices in a mesh: src: 8 (over z), tgt: 32 (over y, x, core).
Axes of the slice: x: 4, y: 4, z: 8, core: 2. Of those that a mesh axis runs over, the one named last changes fastest.
Arguments:
- src_feat: float32 [16, 32768], P(None, ('src', 'tgt')), may hold values from -1.5 to 16
- tgt_feat: float32 [16, 32768], P(None, ('tgt', 'src')), may hold values from -1.5 to 1.5
- src_mass: float32 [32768], P(('src', 'tgt')), may hold values from 0.2 to 6
- tgt_mass: float32 [32768], P(('tgt', 'src')), may hold values from 0.2 to 6
- g_init: float32 [32768], P('tgt'), may hold values from -3 to 3
Outputs:
- source_potential: float32 [32768], P(('src', 'tgt'))
- target_potential: float32 [32768], P('tgt')
- bary_map: float32 [16, 32768], P(None, ('src', 'tgt'))
The draws below stay inside these ranges and needn't reach their ends.
All inputs are finite; a program needn't handle non-finite values.
Results may differ from the reference program's by a relative error of at most 0.0003.
Values sent between devices are 32-bit elements; how exact they have to be, the bound alone decides.
No kernel may reach another device: no remote copies, remote signals or barrier semaphores. Data moves between devices by JAX's collectives and lax.ppermute only.
A program may use at most 64 MiB of HBM per device.

```python
import math
import jax
import jax.numpy as jnp
from jax import lax

F = 16
NS = 32768
NT = 32768


def mass_draw(key, count, lower, upper):
    ramp = 1.0 + 2.0 * jnp.arange(count, dtype=jnp.float32) / max(count - 1, 1)
    return jax.random.uniform(key, (count,), jnp.float32, lower, upper) * ramp


def draw_src_mass(key, part):
    key = jax.random.fold_in(key, 3)
    return mass_draw(key, NS, 0.5, 1.5)


def draw_tgt_mass(key, part):
    key = jax.random.fold_in(key, 4)
    return mass_draw(key, NT, 0.5, 1.5)


def draw_src_feat(key, part):
    key = jax.random.fold_in(key, 1)
    first = jax.random.fold_in(key, 0)
    return jnp.clip(0.25 * jax.random.normal(first, (F, NS), jnp.float32), -1.5, 1.5)


def draw_tgt_feat(key, part):
    key = jax.random.fold_in(key, 2)
    return jnp.clip(0.25 * jax.random.normal(key, (F, NT), jnp.float32), -1.5, 1.5)


def shard_levels(key, shape, pieces, low, top_value):
    loudness, own = 1.0, jax.random.fold_in(key, 6)
    for axis_at, parts in pieces:
        steps = jnp.exp(jax.random.uniform(jax.random.fold_in(own, axis_at), (parts,), jnp.float32, low / len(pieces), top_value / len(pieces)))
        loudness = loudness * jnp.repeat(steps, shape[axis_at] // parts).reshape([-1 if axis == axis_at else 1 for axis in range(len(shape))])
    return loudness


def noise(rng, extent, scale, limit, shards=(), kind=jnp.bfloat16):
    gain = shard_levels(rng, extent, shards, -0.22, 0.18) if shards else 1.0
    values = jax.random.normal(rng, extent, jnp.float32) * scale * gain
    return jnp.minimum(jnp.maximum(values, -limit), limit).astype(kind)


def setup_inputs(seed: int = 0) -> dict:
    splits = jax.random.split(jax.random.key(seed), 6)
    return {
        "src_feat": draw_src_feat(jax.random.fold_in(splits[5], 71), 0),
        "tgt_feat": draw_tgt_feat(jax.random.fold_in(splits[5], 71), 0),
        "src_mass": draw_src_mass(jax.random.fold_in(splits[5], 71), 0),
        "tgt_mass": draw_tgt_mass(jax.random.fold_in(splits[5], 71), 0),
        "g_init": noise(splits[4], (NT,), 0.5, 3.0, ((0, 32),), jnp.float32),
    }


epsilon = 0.5


def cost_block(block, others):
    cross = jnp.einsum('fi,fj->ij', block, others, precision=lax.Precision.HIGHEST)
    return jnp.sum(block * block, 0)[:, None] + jnp.sum(others * others, 0)[None, :] - 2.0 * cross


def split_blocks(feats):
    width, count = feats.shape
    size = math.gcd(count, 1024)
    return feats.reshape(width, count // size, size).transpose(1, 0, 2)


def row_lse(feats, others, potential):
    def one_block(block):
        scores = (potential[None, :] - cost_block(block, others)) / epsilon
        top = jnp.max(scores, 1)
        return top + jnp.log(jnp.sum(jnp.exp(scores - top[:, None]), 1))
    return lax.map(one_block, split_blocks(feats)).reshape(feats.shape[1])


def reference(src_feat, tgt_feat, src_mass, tgt_mass, g_init):
    log_a = jnp.log(src_mass / jnp.sum(src_mass))
    log_b = jnp.log(tgt_mass / jnp.sum(tgt_mass))
    first_f = epsilon * log_a - epsilon * row_lse(src_feat, tgt_feat, g_init)
    target_potential = epsilon * log_b - epsilon * row_lse(tgt_feat, src_feat, first_f)
    source_potential = epsilon * log_a - epsilon * row_lse(src_feat, tgt_feat, target_potential)
    count = src_feat.shape[1]
    size = math.gcd(count, 1024)
    pot_blocks = source_potential.reshape(count // size, size)
    mass_blocks = log_a.reshape(count // size, size)

    def one_block(items):
        block, pot_rows, mass_rows = items
        weights = jnp.exp((pot_rows[:, None] + target_potential[None, :] - cost_block(block, tgt_feat)) / epsilon - mass_rows[:, None])
        return jnp.einsum('ij,fj->fi', weights, tgt_feat, precision=lax.Precision.HIGHEST)

    sums = lax.map(one_block, (split_blocks(src_feat), pot_blocks, mass_blocks))
    bary_map = sums.transpose(1, 0, 2).reshape(src_feat.shape[0], count)
    return source_potential, target_potential, bary_map
```

```python
import functools

import jax
import jax.numpy as jnp
from jax import lax
from jax.experimental import pallas as pl
from jax.experimental.pallas import tpu as pltpu
from jax.sharding import Mesh, PartitionSpec as P

f32 = jnp.float32
bf16 = jnp.bfloat16
LOG2E = 1.4426950408889634
LN2 = 0.6931471805599453
epsilon = 0.5
UNIT = LOG2E / epsilon

T_ORDER = (0, 0, 1, 0, 1, 2)
S_ORDER = (0, 1, 0, 2, 1, 0)
COLS = ("z", "x")
ROWS = ("y", "c")


def split3(v):
    hi = v.astype(bf16)
    rest = v - hi.astype(f32)
    mid = rest.astype(bf16)
    return hi, mid, (rest - mid.astype(f32)).astype(bf16)


def bias_rows(row):
    hi, mid, lo = (jnp.broadcast_to(p.astype(f32), (16, 128)) for p in split3(row))
    r = lax.broadcasted_iota(jnp.int32, (16, 128), 0)
    return jnp.where(r == 0, hi, jnp.where(r == 1, mid, jnp.where(r == 2, lo, 0.0))).astype(bf16)


def put_feats(aug, k, feats, order):
    pieces = split3(feats)
    for at, which in enumerate(order):
        aug[at * 16 : at * 16 + 16, k * 128 : k * 128 + 128] = pieces[which]


def fill_tgt(aug, tall, bias):
    aug[112:128, :] = jnp.ones((16, aug.shape[1]), bf16)
    for k in range(tall.shape[0]):
        put_feats(aug, k, tall[k, 0:16, :], T_ORDER)
        if bias is not None:
            aug[96:112, k * 128 : k * 128 + 128] = bias_rows(bias(k))
    if bias is None:
        aug[96:112, :] = jnp.zeros((16, aug.shape[1]), bf16)


def fill_src(aug, turned, sall, bias):
    aug[96:112, :] = jnp.ones((16, aug.shape[1]), bf16)
    for k in range(sall.shape[0]):
        put_feats(aug, k, sall[k, 0:16, :] * (2.0 * UNIT), S_ORDER)
        if bias is not None:
            aug[112:128, k * 128 : k * 128 + 128] = bias_rows(bias(k))
    if bias is None:
        aug[112:128, :] = jnp.zeros((16, aug.shape[1]), bf16)
    for k in range(sall.shape[0]):
        turned[k * 128 : k * 128 + 128, :] = aug[:, k * 128 : k * 128 + 128].T


def lse2(parts):
    top = jnp.max(parts, 0)
    return top + jnp.log2(jnp.sum(jnp.exp2(parts - top[None]), 0))


def total(rows):
    return jnp.sum(jnp.sum(rows, 0, keepdims=True), 1, keepdims=True)


def pack_body(zat, src_feat, tgt_feat, src_mass, tgt_mass, g, tmsg, smsg):
    g_own = g[pl.ds(zat[0], 1), :]
    for k in range(tmsg.shape[0]):
        tmsg[k, 0:16, :] = tgt_feat[...]
        tmsg[k, 16:17, :] = g_own
        tmsg[k, 17:18, :] = tgt_mass[...]
        tmsg[k, 18:19, :] = src_mass[...]
    for k in range(smsg.shape[0]):
        smsg[k, 0:16, :] = src_feat[...]
        smsg[k, 16:17, :] = src_mass[...]


def first_body(tall, sall, out, taug, saug, turned):
    def bias(k):
        y = tall[k, 0:16, :]
        return UNIT * (tall[k, 16:17, :] - jnp.sum(y * y, 0, keepdims=True))

    fill_tgt(taug, tall, bias)
    fill_src(saug, turned, sall, None)
    n = out.shape[0]
    for r in range(sall.shape[0]):
        v = lax.dot(turned[r * 128 : r * 128 + 128, :], taug[...], preferred_element_type=f32)
        top = jnp.max(v, 1, keepdims=True)
        s = jnp.sum(jnp.exp2(v - top), 1, keepdims=True)
        line = jnp.broadcast_to(top + jnp.log2(s), (128, 128)).T[0:1, :]
        for d in range(n):
            out[d, r : r + 1, :] = line
    tmass = jnp.sum(tall[:, 17, :], 0, keepdims=True)
    smass = jnp.sum(tall[:, 18, :], 0, keepdims=True)
    for d in range(n):
        out[d, 8:9, :] = smass
        out[d, 9:10, :] = tmass


def second_body(part, tall, sall, out, taug, saug, turned):
    lse = lse2(part[:, 0:8, :])

    def bias(k):
        return jnp.log2(sall[k, 16:17, :]) - lse[k : k + 1, :]

    fill_tgt(taug, tall, None)
    fill_src(saug, turned, sall, bias)
    for c in range(taug.shape[1] // 256):
        v = lax.dot(turned[...], taug[:, c * 256 : c * 256 + 256], preferred_element_type=f32)
        v = v.reshape(v.shape[0] // 8, 8, 256)
        top = jnp.max(v, 0)
        s = jnp.sum(jnp.exp2(v - top[None]), 0)
        most = jnp.max(top, 0, keepdims=True)
        s = jnp.sum(s * jnp.exp2(top - most), 0, keepdims=True)
        line = most + jnp.log2(s)
        for d in range(out.shape[0]):
            out[d, 2 * c : 2 * c + 1, :] = line[:, :128]
            out[d, 2 * c + 1 : 2 * c + 2, :] = line[:, 128:]


def third_body(xat, part, first, tall, sall, out, pot, taug, saug, turned, held):
    held[...] = jnp.log2(tall[:, 17, :]) - lse2(part[...])
    fill_tgt(taug, tall, lambda k: held[k : k + 1, :])
    fill_src(saug, turned, sall, None)
    for r in range(sall.shape[0]):
        v = lax.dot(turned[r * 128 : r * 128 + 128, :], taug[...], preferred_element_type=f32)
        top = jnp.max(v, 1, keepdims=True)
        w = jnp.exp2(v - top)
        hi = w.astype(bf16)
        lo = (w - hi.astype(f32)).astype(bf16)
        dims = (((1,), (1,)), ((), ()))
        acc = lax.dot_general(hi, taug[...], dims, preferred_element_type=f32)
        acc = acc + lax.dot_general(lo, taug[...], dims, preferred_element_type=f32)
        acc = acc.T
        s = acc[112:113, :]
        out[r, 0:16, :] = (acc[0:16, :] + acc[32:48, :] + acc[80:96, :]) / s
        out[r, 16:17, :] = jnp.broadcast_to(top, (128, 128)).T[0:1, :] + jnp.log2(s)
    shift = jnp.log2(total(first[:, 8, :])) - jnp.log2(total(first[:, 9, :]))
    for z in range(pot.shape[0]):
        at = 4 * z + xat[0]
        y = tall[pl.ds(at, 1), 0:16, :][0]
        pot[z : z + 1, :] = (held[pl.ds(at, 1), :] + shift) / UNIT + jnp.sum(y * y, 0, keepdims=True)


def last_body(part, first, feat, mass, pot, bary):
    lses = part[:, 16, :]
    top = jnp.max(lses, 0, keepdims=True)
    w = jnp.exp2(lses - top)
    s = jnp.sum(w, 0, keepdims=True)
    acc = jnp.zeros((16, 128), f32)
    for k in range(part.shape[0]):
        acc = acc + part[k, 0:16, :] * w[k : k + 1, :]
    bary[...] = acc / s
    shift = jnp.log2(total(first[:, 9, :])) - 2.0 * jnp.log2(total(first[:, 8, :]))
    x = feat[...]
    lse = top + jnp.log2(s)
    pot[...] = (jnp.log2(mass[...]) - lse + shift) / UNIT + jnp.sum(x * x, 0, keepdims=True)


def call(body, outs, args, scratch=(), scalars=0):
    vmem = pl.BlockSpec(memory_space=pltpu.VMEM)
    smem = pl.BlockSpec(memory_space=pltpu.SMEM)
    return pl.pallas_call(
        body,
        out_shape=[jax.ShapeDtypeStruct(s, f32) for s in outs],
        in_specs=[smem] * scalars + [vmem] * (len(args) - scalars),
        out_specs=[vmem] * len(outs),
        scratch_shapes=list(scratch),
        compiler_params=pltpu.CompilerParams(vmem_limit_bytes=48 << 20),
    )(*args)


def exchange(v, axes):
    return lax.all_to_all(v, axes, 0, 0, tiled=True)


def local(src_feat, tgt_feat, src_mass, tgt_mass, g_init):
    zat = lax.axis_index("z").reshape(1)
    xat = lax.axis_index("x").reshape(1)
    smass = src_mass.reshape(1, 128)
    nt, ns = 32, 8
    aug = [pltpu.VMEM((128, nt * 128), bf16), pltpu.VMEM((128, ns * 128), bf16), pltpu.VMEM((ns * 128, 128), bf16)]
    tmsg, smsg = call(
        pack_body,
        [(nt, 19, 128), (ns, 17, 128)],
        (zat, src_feat, tgt_feat, smass, tgt_mass.reshape(1, 128), g_init.reshape(8, 128)),
        scalars=1,
    )
    tall = exchange(tmsg, COLS)
    sall = exchange(smsg, ROWS)
    (msg,) = call(first_body, [(ns, 10, 128)], (tall, sall), aug)
    first = exchange(msg, ROWS)
    (msg,) = call(second_body, [(nt, nt, 128)], (first, tall, sall), aug)
    second = exchange(msg, COLS)
    msg, tgt_pot = call(
        third_body,
        [(ns, 17, 128), (8, 128)],
        (xat, second, first, tall, sall),
        aug + [pltpu.VMEM((nt, 128), f32)],
        scalars=1,
    )
    third = exchange(msg, ROWS)
    src_pot, bary = call(last_body, [(1, 128), (16, 128)], (third, first, src_feat, smass))
    return src_pot.reshape(128), tgt_pot.reshape(1024), bary


def solution(mesh):
    axes = ("z", "y", "x", "c")
    split = Mesh(mesh.devices.reshape(8, 4, 4, 2), axes)
    src, tgt = ("z", "y", "x", "c"), ("y", "x", "c", "z")
    return jax.shard_map(
        local,
        mesh=split,
        in_specs=(P(None, src), P(None, tgt), P(src), P(tgt), P(("y", "x", "c"))),
        out_specs=(P(src), P(("y", "x", "c")), P(None, src)),
        check_vma=False,
    )
```

```python
import functools

import jax
import jax.numpy as jnp
from jax import lax
from jax.experimental import pallas as pl
from jax.experimental.pallas import tpu as pltpu
from jax.sharding import Mesh, PartitionSpec as P

f32 = jnp.float32
bf16 = jnp.bfloat16
LOG2E = 1.4426950408889634
LN2 = 0.6931471805599453
epsilon = 0.5
UNIT = LOG2E / epsilon

T_ORDER = (0, 0, 1, 0, 1, 2)
S_ORDER = (0, 1, 0, 2, 1, 0)
COLS = ("z", "x")
ROWS = ("y", "c")


def split3(v):
    hi = v.astype(bf16)
    rest = v - hi.astype(f32)
    mid = rest.astype(bf16)
    return hi, mid, (rest - mid.astype(f32)).astype(bf16)


def bias_rows(row):
    hi, mid, lo = (jnp.broadcast_to(p.astype(f32), (16, 128)) for p in split3(row))
    r = lax.broadcasted_iota(jnp.int32, (16, 128), 0)
    return jnp.where(r == 0, hi, jnp.where(r == 1, mid, jnp.where(r == 2, lo, 0.0))).astype(bf16)


def put_feats(aug, k, feats, order):
    pieces = split3(feats)
    for at, which in enumerate(order):
        aug[at * 16 : at * 16 + 16, k * 128 : k * 128 + 128] = pieces[which]


def fill_tgt(aug, turned, tall, bias):
    n = tall.shape[0]
    aug[112:128, :] = jnp.ones((16, n * 128), bf16)
    if bias is None:
        aug[96:112, :] = jnp.zeros((16, n * 128), bf16)
    for k in range(n):
        put_feats(aug, k, tall[k, 0:16, :], T_ORDER)
        if bias is not None:
            aug[96:112, k * 128 : k * 128 + 128] = bias_rows(bias(k))
            turned[k * 128 : k * 128 + 128, :] = aug[:, k * 128 : k * 128 + 128].T


def fill_src(aug, turned, sall, bias):
    n = sall.shape[0]
    aug[96:112, :] = jnp.ones((16, n * 128), bf16)
    if bias is None:
        aug[112:128, :] = jnp.zeros((16, n * 128), bf16)
    for k in range(n):
        put_feats(aug, k, sall[k, 0:16, :] * (2.0 * UNIT), S_ORDER)
        if bias is not None:
            aug[112:128, k * 128 : k * 128 + 128] = bias_rows(bias(k))
            turned[k * 128 : k * 128 + 128, :] = aug[:, k * 128 : k * 128 + 128].T


def scores(lhs, rhs):
    return lax.dot(lhs, rhs, preferred_element_type=f32)


def sample_top(lhs, rhs, groups):
    rows = lhs.shape[0] // groups
    some = jnp.concatenate([lhs[g * rows : g * rows + 16, :] for g in range(groups)], 0)
    return jnp.max(scores(some, rhs), 0, keepdims=True)


def full_top(lhs, rhs):
    def step(k, top):
        v = scores(lhs[pl.ds(pl.multiple_of(k * 256, 256), 256), :], rhs)
        return jnp.maximum(top, jnp.max(v, 0, keepdims=True))

    return lax.fori_loop(0, lhs.shape[0] // 256, step, jnp.full((1, rhs.shape[1]), -3e38, f32))


def in_range(sums):
    ok = jnp.ones((1, 256), f32)
    for s in sums:
        ok = jnp.minimum(ok, jnp.where(s < 2.0**100, 1.0, 0.0))
    return jnp.min(ok) > 0.5


def lse_blocks(lhs, aug, groups, put):
    blocks = aug.shape[1] // 256
    tops = [sample_top(lhs, aug[:, c * 256 : c * 256 + 256], groups) for c in range(blocks)]
    sums = []
    for c in range(blocks):
        v = scores(lhs[...], aug[:, c * 256 : c * 256 + 256]).reshape(lhs.shape[0] // 8, 8, 256)
        s = jnp.sum(jnp.sum(jnp.exp2(v - tops[c][None]), 0), 0, keepdims=True)
        put(c, tops[c] + jnp.log2(s))
        sums.append(s)

    @pl.when(jnp.logical_not(in_range(sums)))
    def _():
        @pl.loop(0, blocks)
        def _(c):
            rhs = aug[:, pl.ds(pl.multiple_of(c * 256, 256), 256)]
            top = full_top(lhs, rhs)

            def step(k, s):
                v = scores(lhs[pl.ds(pl.multiple_of(k * 256, 256), 256), :], rhs)
                return s + jnp.sum(jnp.exp2(v - top), 0, keepdims=True)

            s = lax.fori_loop(0, lhs.shape[0] // 256, step, jnp.zeros((1, 256), f32))
            put(c, top + jnp.log2(s))


def lse2(parts):
    top = jnp.max(parts, 0)
    return top + jnp.log2(jnp.sum(jnp.exp2(parts - top[None]), 0))


def total(rows):
    return jnp.sum(jnp.sum(rows, 0, keepdims=True), 1, keepdims=True)


def pack_body(zat, src_feat, tgt_feat, src_mass, tgt_mass, g, tmsg, smsg):
    g_own = g[pl.ds(zat[0], 1), :]
    for k in range(tmsg.shape[0]):
        tmsg[k, 0:16, :] = tgt_feat[...]
        tmsg[k, 16:17, :] = g_own
        tmsg[k, 17:18, :] = tgt_mass[...]
        tmsg[k, 18:19, :] = src_mass[...]
    for k in range(smsg.shape[0]):
        smsg[k, 0:16, :] = src_feat[...]
        smsg[k, 16:17, :] = src_mass[...]


def put_line(out):
    def put(c, line):
        for d in range(out.shape[0]):
            out[d, pl.ds(2 * c, 1), :] = line[:, :128]
            out[d, pl.ds(2 * c + 1, 1), :] = line[:, 128:]

    return put


def first_body(tall, sall, out, taug, tturn, saug):
    def bias(k):
        y = tall[k, 0:16, :]
        return UNIT * (tall[k, 16:17, :] - jnp.sum(y * y, 0, keepdims=True))

    fill_tgt(taug, tturn, tall, bias)
    fill_src(saug, None, sall, None)
    lse_blocks(tturn, saug, 16, put_line(out))
    tmass = jnp.sum(tall[:, 17, :], 0, keepdims=True)
    smass = jnp.sum(tall[:, 18, :], 0, keepdims=True)
    for d in range(out.shape[0]):
        out[d, 8:9, :] = smass
        out[d, 9:10, :] = tmass


def second_body(part, tall, sall, out, taug, saug, sturn):
    lse = lse2(part[:, 0:8, :])

    def bias(k):
        return jnp.log2(sall[k, 16:17, :]) - lse[k : k + 1, :]

    fill_tgt(taug, None, tall, None)
    fill_src(saug, sturn, sall, bias)
    lse_blocks(sturn, taug, 4, put_line(out))


def weigh(lhs, taug_rows, rhs, top):
    w = jnp.exp2(scores(lhs, rhs) - top)
    hi = w.astype(bf16)
    lo = (w - hi.astype(f32)).astype(bf16)
    return scores(taug_rows, hi) + scores(taug_rows, lo)


def third_body(xat, part, first, tall, sall, out, pot, taug, tturn, saug, held):
    held[...] = jnp.log2(tall[:, 17, :]) - lse2(part[...])
    fill_tgt(taug, tturn, tall, lambda k: held[k : k + 1, :])
    fill_src(saug, None, sall, None)
    def put(c, acc, top):
        s = acc[64:65, :]
        feats = (acc[0:16, :] + acc[16:32, :] + acc[48:64, :]) / s
        lse = top + jnp.log2(s)
        for h in range(2):
            out[2 * c + h, 0:16, :] = feats[:, h * 128 : h * 128 + 128]
            out[2 * c + h, 16:17, :] = lse[:, h * 128 : h * 128 + 128]

    def rows_of(at, n):
        return jnp.concatenate([taug[32:96, pl.ds(at, n)], taug[112:128, pl.ds(at, n)]], 0)

    blocks, count = saug.shape[1] // 256, tturn.shape[0]
    tops = [sample_top(tturn, saug[:, c * 256 : c * 256 + 256], 16) for c in range(blocks)]
    sums = []
    for c in range(blocks):
        rhs = saug[:, c * 256 : c * 256 + 256]
        acc = jnp.zeros((80, 256), f32)
        for k in range(count // 1024):
            acc = acc + weigh(tturn[k * 1024 : k * 1024 + 1024, :], rows_of(k * 1024, 1024), rhs, tops[c])
        put(c, acc, tops[c])
        sums.append(acc[64:65, :])

    @pl.when(jnp.logical_not(in_range(sums)))
    def _():
        @pl.loop(0, blocks)
        def _(c):
            rhs = saug[:, pl.ds(pl.multiple_of(c * 256, 256), 256)]
            top = full_top(tturn, rhs)

            def step(k, acc):
                at = pl.multiple_of(k * 256, 256)
                return acc + weigh(tturn[pl.ds(at, 256), :], rows_of(at, 256), rhs, top)

            put(c, lax.fori_loop(0, count // 256, step, jnp.zeros((80, 256), f32)), top)

    shift = jnp.log2(total(first[:, 8, :])) - jnp.log2(total(first[:, 9, :]))
    for z in range(pot.shape[0]):
        at = 4 * z + xat[1]
        y = tall[pl.ds(at, 1), 0:16, :][0]
        pot[z : z + 1, :] = (held[pl.ds(at, 1), :] + shift) / UNIT + jnp.sum(y * y, 0, keepdims=True)


def last_body(part, first, feat, mass, pot, bary):
    lses = part[:, 16, :]
    top = jnp.max(lses, 0, keepdims=True)
    w = jnp.exp2(lses - top)
    s = jnp.sum(w, 0, keepdims=True)
    acc = jnp.zeros((16, 128), f32)
    for k in range(part.shape[0]):
        acc = acc + part[k, 0:16, :] * w[k : k + 1, :]
    bary[...] = acc / s
    shift = jnp.log2(total(first[:, 9, :])) - 2.0 * jnp.log2(total(first[:, 8, :]))
    x = feat[...]
    lse = top + jnp.log2(s)
    pot[...] = (jnp.log2(mass[...]) - lse + shift) / UNIT + jnp.sum(x * x, 0, keepdims=True)


def call(body, outs, args, scratch=(), scalars=0):
    vmem = pl.BlockSpec(memory_space=pltpu.VMEM)
    smem = pl.BlockSpec(memory_space=pltpu.SMEM)
    return pl.pallas_call(
        body,
        out_shape=[jax.ShapeDtypeStruct(s, f32) for s in outs],
        in_specs=[smem] * scalars + [vmem] * (len(args) - scalars),
        out_specs=[vmem] * len(outs),
        scratch_shapes=list(scratch),
        compiler_params=pltpu.CompilerParams(vmem_limit_bytes=48 << 20),
    )(*args)


def exchange(v, axes):
    return lax.all_to_all(v, axes, 0, 0, tiled=True)


def local(src_feat, tgt_feat, src_mass, tgt_mass, g_init):
    at = jnp.stack([lax.axis_index("z"), lax.axis_index("x")])
    smass = src_mass.reshape(1, 128)
    nt, ns = 32, 8
    taug, tturn = pltpu.VMEM((128, nt * 128), bf16), pltpu.VMEM((nt * 128, 128), bf16)
    saug, sturn = pltpu.VMEM((128, ns * 128), bf16), pltpu.VMEM((ns * 128, 128), bf16)
    tmsg, smsg = call(
        pack_body,
        [(nt, 19, 128), (ns, 17, 128)],
        (at, src_feat, tgt_feat, smass, tgt_mass.reshape(1, 128), g_init.reshape(8, 128)),
        scalars=1,
    )
    tall = exchange(tmsg, COLS)
    sall = exchange(smsg, ROWS)
    (msg,) = call(first_body, [(ns, 10, 128)], (tall, sall), [taug, tturn, saug])
    first = exchange(msg, ROWS)
    (msg,) = call(second_body, [(nt, nt, 128)], (first, tall, sall), [taug, saug, sturn])
    second = exchange(msg, COLS)
    msg, tgt_pot = call(
        third_body,
        [(ns, 17, 128), (8, 128)],
        (at, second, first, tall, sall),
        [taug, tturn, saug, pltpu.VMEM((nt, 128), f32)],
        scalars=1,
    )
    third = exchange(msg, ROWS)
    src_pot, bary = call(last_body, [(1, 128), (16, 128)], (third, first, src_feat, smass))
    return src_pot.reshape(128), tgt_pot.reshape(1024), bary


def solution(mesh):
    axes = ("z", "y", "x", "c")
    split = Mesh(mesh.devices.reshape(8, 4, 4, 2), axes)
    src, tgt = ("z", "y", "x", "c"), ("y", "x", "c", "z")
    return jax.shard_map(
        local,
        mesh=split,
        in_specs=(P(None, src), P(None, tgt), P(src), P(tgt), P(("y", "x", "c"))),
        out_specs=(P(src), P(("y", "x", "c")), P(None, src)),
        check_vma=False,
    )
```

```python
import functools

import jax
import jax.numpy as jnp
from jax import lax
from jax.experimental import pallas as pl
from jax.experimental.pallas import tpu as pltpu
from jax.sharding import Mesh, PartitionSpec as P

f32 = jnp.float32
bf16 = jnp.bfloat16
LOG2E = 1.4426950408889634
LN2 = 0.6931471805599453
epsilon = 0.5
UNIT = LOG2E / epsilon

T_ORDER = (0, 0, 1, 0, 1, 2)
S_ORDER = (0, 1, 0, 2, 1, 0)
COLS = ("z", "c")
ROWS = ("y", "x")


def split3(v):
    hi = v.astype(bf16)
    rest = v - hi.astype(f32)
    mid = rest.astype(bf16)
    return hi, mid, (rest - mid.astype(f32)).astype(bf16)


def bias_rows(row):
    hi, mid, lo = (jnp.broadcast_to(p.astype(f32), (16, 128)) for p in split3(row))
    r = lax.broadcasted_iota(jnp.int32, (16, 128), 0)
    return jnp.where(r == 0, hi, jnp.where(r == 1, mid, jnp.where(r == 2, lo, 0.0))).astype(bf16)


def put_feats(aug, k, feats, order):
    pieces = split3(feats)
    for at, which in enumerate(order):
        aug[at * 16 : at * 16 + 16, k * 128 : k * 128 + 128] = pieces[which]


def fill_tgt(aug, turned, tall, bias):
    n = tall.shape[0]
    aug[112:128, :] = jnp.ones((16, n * 128), bf16)
    if bias is None:
        aug[96:112, :] = jnp.zeros((16, n * 128), bf16)
    for k in range(n):
        put_feats(aug, k, tall[k, 0:16, :], T_ORDER)
        if bias is not None:
            aug[96:112, k * 128 : k * 128 + 128] = bias_rows(bias(k))
            turned[k * 128 : k * 128 + 128, :] = aug[:, k * 128 : k * 128 + 128].T


def place(k):
    def pos(to, own):
        step = (to - own + 4) % 4
        return jnp.where(step == 0, 0, jnp.where(step == 1, 2, jnp.where(step == 2, 3, 1)))

    return pos(k // 4, lax.axis_index("y")) * 4 + pos(k % 4, lax.axis_index("x"))


def fill_src(aug, turned, sall, bias):
    n = sall.shape[0]
    aug[96:112, :] = jnp.ones((16, n * 128), bf16)
    if bias is None:
        aug[112:128, :] = jnp.zeros((16, n * 128), bf16)
    for k in range(n):
        put_feats(aug, k, sall[place(k), 0:16, :] * (2.0 * UNIT), S_ORDER)
        if bias is not None:
            aug[112:128, k * 128 : k * 128 + 128] = bias_rows(bias(k))
            turned[k * 128 : k * 128 + 128, :] = aug[:, k * 128 : k * 128 + 128].T


def scores(lhs, rhs):
    return lax.dot(lhs, rhs, preferred_element_type=f32)


def sample_top(lhs, rhs, groups):
    rows = lhs.shape[0] // groups
    some = jnp.concatenate([lhs[g * rows : g * rows + 16, :] for g in range(groups)], 0)
    return jnp.max(scores(some, rhs), 0, keepdims=True)


def full_top(lhs, rhs):
    def step(k, top):
        v = scores(lhs[pl.ds(pl.multiple_of(k * 256, 256), 256), :], rhs)
        return jnp.maximum(top, jnp.max(v, 0, keepdims=True))

    return lax.fori_loop(0, lhs.shape[0] // 256, step, jnp.full((1, rhs.shape[1]), -3e38, f32))


def in_range(sums):
    ok = jnp.ones((1, 256), f32)
    for s in sums:
        ok = jnp.minimum(ok, jnp.where(s < 2.0**100, 1.0, 0.0))
    return jnp.min(ok) > 0.5


def lse_blocks(lhs, aug, put):
    blocks, groups = aug.shape[1] // 256, lhs.shape[0] // 256
    tops = [sample_top(lhs, aug[:, c * 256 : c * 256 + 256], groups) for c in range(blocks)]
    sums = []
    for c in range(blocks):
        v = scores(lhs[...], aug[:, c * 256 : c * 256 + 256]).reshape(lhs.shape[0] // 8, 8, 256)
        s = jnp.sum(jnp.sum(jnp.exp2(v - tops[c][None]), 0), 0, keepdims=True)
        put(c, tops[c] + jnp.log2(s))
        sums.append(s)

    @pl.when(jnp.logical_not(in_range(sums)))
    def _():
        @pl.loop(0, blocks)
        def _(c):
            rhs = aug[:, pl.ds(pl.multiple_of(c * 256, 256), 256)]
            top = full_top(lhs, rhs)

            def step(k, s):
                v = scores(lhs[pl.ds(pl.multiple_of(k * 256, 256), 256), :], rhs)
                return s + jnp.sum(jnp.exp2(v - top), 0, keepdims=True)

            s = lax.fori_loop(0, lhs.shape[0] // 256, step, jnp.zeros((1, 256), f32))
            put(c, top + jnp.log2(s))


def lse2(parts):
    top = jnp.max(parts, 0)
    return top + jnp.log2(jnp.sum(jnp.exp2(parts - top[None]), 0))


def total(rows):
    return jnp.sum(jnp.sum(rows, 0, keepdims=True), 1, keepdims=True)


def pack_body(*refs):
    ins, tmsg, held, sems = refs[:4], refs[4], refs[5:9], refs[9]
    copies = [pltpu.make_async_copy(a, b, sems.at[n]) for n, (a, b) in enumerate(zip(ins, held))]
    for copy in copies:
        copy.start()
    for copy in copies:
        copy.wait()
    tgt_feat, src_mass, tgt_mass, g = held
    g_own = g[pl.ds(lax.axis_index("z"), 1), :]
    for k in range(tmsg.shape[0]):
        tmsg[k, 0:16, :] = tgt_feat[...]
        tmsg[k, 16:17, :] = g_own
        tmsg[k, 17:18, :] = tgt_mass[...]
        tmsg[k, 18:19, :] = src_mass[...]


def put_line(out):
    def put(c, line):
        for d in range(out.shape[0]):
            out[d, pl.ds(2 * c, 1), :] = line[:, :128]
            out[d, pl.ds(2 * c + 1, 1), :] = line[:, 128:]

    return put


def first_body(tall, sall, mass, out, taug, tturn, saug):
    def bias(k):
        y = tall[k, 0:16, :]
        return UNIT * (tall[k, 16:17, :] - jnp.sum(y * y, 0, keepdims=True))

    fill_tgt(taug, tturn, tall, bias)
    fill_src(saug, None, sall, None)
    lse_blocks(tturn, saug, put_line(out))
    for d in range(out.shape[0]):
        out[d, 16:17, :] = mass[...]


def second_body(part, tall, sall, out, taug, saug, sturn):
    lse = lse2(part[:, 0:16, :])

    def bias(k):
        return jnp.log2(part[k, 16:17, :]) - lse[k : k + 1, :]

    fill_tgt(taug, None, tall, None)
    fill_src(saug, sturn, sall, bias)
    lse_blocks(sturn, taug, put_line(out))


def weigh(lhs, taug_rows, rhs, top):
    w = jnp.exp2(scores(lhs, rhs) - top)
    hi = w.astype(bf16)
    lo = (w - hi.astype(f32)).astype(bf16)
    return scores(taug_rows, hi) + scores(taug_rows, lo)


def third_body(part, tall, sall, out, pot, taug, tturn, saug, held):
    held[...] = jnp.log2(tall[:, 17, :]) - lse2(part[...])
    fill_tgt(taug, tturn, tall, lambda k: held[k : k + 1, :])
    fill_src(saug, None, sall, None)
    def put(c, acc, top):
        s = acc[64:65, :]
        feats = (acc[0:16, :] + acc[16:32, :] + acc[48:64, :]) / s
        lse = top + jnp.log2(s)
        for h in range(2):
            out[2 * c + h, 0:16, :] = feats[:, h * 128 : h * 128 + 128]
            out[2 * c + h, 16:17, :] = lse[:, h * 128 : h * 128 + 128]

    def rows_of(at, n):
        return jnp.concatenate([taug[32:96, pl.ds(at, n)], taug[112:128, pl.ds(at, n)]], 0)

    blocks, count = saug.shape[1] // 256, tturn.shape[0]
    tops = [sample_top(tturn, saug[:, c * 256 : c * 256 + 256], count // 256) for c in range(blocks)]
    sums = []
    for c in range(blocks):
        rhs = saug[:, c * 256 : c * 256 + 256]
        acc = jnp.zeros((80, 256), f32)
        for k in range(count // 1024):
            acc = acc + weigh(tturn[k * 1024 : k * 1024 + 1024, :], rows_of(k * 1024, 1024), rhs, tops[c])
        put(c, acc, tops[c])
        sums.append(acc[64:65, :])

    @pl.when(jnp.logical_not(in_range(sums)))
    def _():
        @pl.loop(0, blocks)
        def _(c):
            rhs = saug[:, pl.ds(pl.multiple_of(c * 256, 256), 256)]
            top = full_top(tturn, rhs)

            def step(k, acc):
                at = pl.multiple_of(k * 256, 256)
                return acc + weigh(tturn[pl.ds(at, 256), :], rows_of(at, 256), rhs, top)

            put(c, lax.fori_loop(0, count // 256, step, jnp.zeros((80, 256), f32)), top)

    masses = [jnp.sum(tall[:, row, :], 0, keepdims=True) for row in (18, 17)]
    for d in range(out.shape[0]):
        out[d, 17:18, :] = masses[0]
        out[d, 18:19, :] = masses[1]
    for z in range(pot.shape[0]):
        k = 2 * z + lax.axis_index("c")
        y = tall[pl.ds(k, 1), 0:16, :][0]
        pot[z : z + 1, :] = held[pl.ds(k, 1), :] / UNIT + jnp.sum(y * y, 0, keepdims=True)


def last_body(part, raw, sall, mass, src_pot, tgt_pot, bary):
    lses = part[:, 16, :]
    top = jnp.max(lses, 0, keepdims=True)
    w = jnp.exp2(lses - top)
    s = jnp.sum(w, 0, keepdims=True)
    acc = jnp.zeros((16, 128), f32)
    for k in range(part.shape[0]):
        acc = acc + part[k, 0:16, :] * w[k : k + 1, :]
    bary[...] = acc / s
    log_a, log_b = jnp.log2(total(part[:, 17, :])), jnp.log2(total(part[:, 18, :]))
    x = sall[0, 0:16, :]
    lse = top + jnp.log2(s)
    src_pot[...] = (jnp.log2(mass[...]) - lse + log_b - 2.0 * log_a) / UNIT + jnp.sum(x * x, 0, keepdims=True)
    tgt_pot[...] = raw[...] + (log_a - log_b) / UNIT


def call(body, outs, args, scratch=(), cost=None, where=pltpu.VMEM, limit=48):
    vmem = pl.BlockSpec(memory_space=pltpu.VMEM)
    return pl.pallas_call(
        body,
        out_shape=[jax.ShapeDtypeStruct(s, f32) for s in outs],
        in_specs=[pl.BlockSpec(memory_space=where)] * len(args),
        out_specs=[vmem] * len(outs),
        scratch_shapes=list(scratch),
        cost_estimate=cost,
        compiler_params=pltpu.CompilerParams(vmem_limit_bytes=limit << 20),
    )(*args)


def exchange(v, axes):
    return lax.all_to_all(v, axes, 0, 0, tiled=True)


def join_body(*refs):
    out, at = refs[-1], 0
    for ref in refs[:-1]:
        out[at : at + ref.shape[0]] = ref[...]
        at += ref.shape[0]


def join(parts, flops):
    shape = (sum(p.shape[0] for p in parts), *parts[0].shape[1:])
    return call(join_body, [shape], parts, cost=pl.CostEstimate(flops=flops, bytes_accessed=1000, transcendentals=0))[0]


def gather_rows(v):
    for axis in ("x", "y"):
        moved = [lax.ppermute(v, axis, [(i, (i + by) % 4) for i in range(4)]) for by in (1, 3, 2)]
        v = join([v, *moved], 10**11) if axis == "x" else jnp.concatenate([v, *moved], 0)
    return v


def local(src_feat, tgt_feat, src_mass, tgt_mass, g_init):
    smass = src_mass.reshape(1, 128)
    nt, ns = 16, 16
    taug, tturn = pltpu.VMEM((128, nt * 128), bf16), pltpu.VMEM((nt * 128, 128), bf16)
    saug, sturn = pltpu.VMEM((128, ns * 128), bf16), pltpu.VMEM((ns * 128, 128), bf16)
    (tmsg,) = call(
        pack_body,
        [(nt, 19, 128)],
        (tgt_feat, smass, tgt_mass.reshape(1, 128), g_init.reshape(8, 128)),
        [pltpu.VMEM(s, f32) for s in ((16, 128), (1, 128), (1, 128), (8, 128))] + [pltpu.SemaphoreType.DMA((4,))],
        where=pltpu.HBM,
        limit=60,
    )
    tall = exchange(tmsg, COLS)
    sall = gather_rows(src_feat.reshape(1, 16, 128))
    (msg,) = call(first_body, [(ns, ns + 1, 128)], (tall, sall, smass), [taug, tturn, saug])
    first = exchange(msg, ROWS)
    (msg,) = call(second_body, [(nt, nt, 128)], (first, tall, sall), [taug, saug, sturn])
    second = exchange(msg, COLS)
    msg, raw = call(
        third_body,
        [(ns, 19, 128), (8, 128)],
        (second, tall, sall),
        [taug, tturn, saug, pltpu.VMEM((nt, 128), f32)],
    )
    third = exchange(msg, ROWS)
    src_pot, tgt_pot, bary = call(last_body, [(1, 128), (8, 128), (16, 128)], (third, raw, sall, smass))
    return src_pot.reshape(128), tgt_pot.reshape(1024), bary


def solution(mesh):
    axes = ("z", "y", "x", "c")
    split = Mesh(mesh.devices.reshape(8, 4, 4, 2), axes)
    src, tgt = ("z", "y", "x", "c"), ("y", "x", "c", "z")
    return jax.shard_map(
        local,
        mesh=split,
        in_specs=(P(None, src), P(None, tgt), P(src), P(tgt), P(("y", "x", "c"))),
        out_specs=(P(src), P(("y", "x", "c")), P(None, src)),
        check_vma=False,
    )
```

```python
import functools

import jax
import jax.numpy as jnp
from jax import lax
from jax.experimental import pallas as pl
from jax.experimental.pallas import tpu as pltpu
from jax.sharding import Mesh, PartitionSpec as P

f32 = jnp.float32
bf16 = jnp.bfloat16
LOG2E = 1.4426950408889634
LN2 = 0.6931471805599453
epsilon = 0.5
UNIT = LOG2E / epsilon

T_ORDER = (0, 0, 1, 0, 1, 2)
S_ORDER = (0, 1, 0, 2, 1, 0)
COLS = ("z", "c")
ROWS = ("y", "x")


def split3(v):
    hi = v.astype(bf16)
    rest = v - hi.astype(f32)
    mid = rest.astype(bf16)
    return hi, mid, (rest - mid.astype(f32)).astype(bf16)


def bias_rows(row):
    hi, mid, lo = (jnp.broadcast_to(p.astype(f32), (16, 128)) for p in split3(row))
    r = lax.broadcasted_iota(jnp.int32, (16, 128), 0)
    return jnp.where(r == 0, hi, jnp.where(r == 1, mid, jnp.where(r == 2, lo, 0.0))).astype(bf16)


def put_feats(aug, k, feats, order):
    pieces = split3(feats)
    for at, which in enumerate(order):
        aug[at * 16 : at * 16 + 16, k * 128 : k * 128 + 128] = pieces[which]


def fill_tgt(aug, turned, tall, bias):
    n = tall.shape[0]
    aug[112:128, :] = jnp.ones((16, n * 128), bf16)
    if bias is None:
        aug[96:112, :] = jnp.zeros((16, n * 128), bf16)
    for k in range(n):
        put_feats(aug, k, tall[k, 0:16, :], T_ORDER)
        if bias is not None:
            aug[96:112, k * 128 : k * 128 + 128] = bias_rows(bias(k))
            turned[k * 128 : k * 128 + 128, :] = aug[:, k * 128 : k * 128 + 128].T


def place(k):
    def pos(to, own):
        step = (to - own + 4) % 4
        return jnp.where(step == 0, 0, jnp.where(step == 1, 2, jnp.where(step == 2, 3, 1)))

    return pos(k // 4, lax.axis_index("y")) * 4 + pos(k % 4, lax.axis_index("x"))


def fill_src(aug, turned, sall, bias):
    n = sall.shape[0]
    aug[96:112, :] = jnp.ones((16, n * 128), bf16)
    if bias is None:
        aug[112:128, :] = jnp.zeros((16, n * 128), bf16)
    for k in range(n):
        put_feats(aug, k, sall[place(k), 0:16, :] * (2.0 * UNIT), S_ORDER)
        if bias is not None:
            aug[112:128, k * 128 : k * 128 + 128] = bias_rows(bias(k))
            turned[k * 128 : k * 128 + 128, :] = aug[:, k * 128 : k * 128 + 128].T


def scores(lhs, rhs):
    return lax.dot(lhs, rhs, preferred_element_type=f32)


def sample_top(lhs, rhs, groups):
    rows = lhs.shape[0] // groups
    some = jnp.concatenate([lhs[g * rows : g * rows + 16, :] for g in range(groups)], 0)
    return jnp.max(scores(some, rhs), 0, keepdims=True)


def full_top(lhs, rhs):
    def step(k, top):
        v = scores(lhs[pl.ds(pl.multiple_of(k * 256, 256), 256), :], rhs)
        return jnp.maximum(top, jnp.max(v, 0, keepdims=True))

    return lax.fori_loop(0, lhs.shape[0] // 256, step, jnp.full((1, rhs.shape[1]), -3e38, f32))


def exact_lse_blocks(lhs, aug, put, keep=None):
    @pl.loop(0, aug.shape[1] // 256)
    def _(c):
        cols = pl.ds(pl.multiple_of(c * 256, 256), 256)
        rhs = aug[:, cols]
        top = full_top(lhs, rhs)

        def step(k, s):
            rows = pl.ds(pl.multiple_of(k * 256, 256), 256)
            e = jnp.exp2(scores(lhs[rows, :], rhs) - top)
            if keep is not None:
                keep[rows, cols] = e
            return s + jnp.sum(e, 0, keepdims=True)

        s = lax.fori_loop(0, lhs.shape[0] // 256, step, jnp.zeros((1, 256), f32))
        put(c, top + jnp.log2(s), top)


def lse2(parts):
    top = jnp.max(parts, 0)
    return top + jnp.log2(jnp.sum(jnp.exp2(parts - top[None]), 0))


def total(rows):
    return jnp.sum(jnp.sum(rows, 0, keepdims=True), 1, keepdims=True)


def first_bias(tall, k):
    y = tall[k, 0:16, :]
    return UNIT * (tall[k, 16:17, :] - jnp.sum(y * y, 0, keepdims=True))


def pack_body(*refs):
    ins, (tmsg, src_feat, src_mass), held, sems = refs[:5], refs[5:8], refs[8:11], refs[11]
    tgt_feat, tgt_mass, g = held
    into = (src_feat.at[0], src_mass, tgt_feat, tgt_mass, g)
    copies = [pltpu.make_async_copy(a, b, sems.at[n]) for n, (a, b) in enumerate(zip(ins, into))]
    for copy in copies:
        copy.start()
    for copy in copies:
        copy.wait()
    g_own = g[pl.ds(lax.axis_index("z"), 1), :]
    for k in range(tmsg.shape[0]):
        tmsg[k, 0:16, :] = tgt_feat[...]
        tmsg[k, 16:17, :] = g_own
        tmsg[k, 17:18, :] = tgt_mass[...]
        tmsg[k, 18:19, :] = src_mass[...]


def put_line(out):
    def put(c, line, top=None):
        for d in range(out.shape[0]):
            out[d, pl.ds(2 * c, 1), :] = line[:, :128]
            out[d, pl.ds(2 * c + 1, 1), :] = line[:, 128:]

    return put


def first_body(tall, sall, mass, out, kept, tops, taug, tturn, saug):
    fill_tgt(taug, tturn, tall, lambda k: first_bias(tall, k))
    fill_src(saug, None, sall, None)

    def put(c, line, top):
        put_line(out)(c, line)
        tops[pl.ds(2 * c, 1), :] = top[:, :128]
        tops[pl.ds(2 * c + 1, 1), :] = top[:, 128:]

    blocks, groups = saug.shape[1] // 256, tturn.shape[0] // 256
    shifts = [sample_top(tturn, saug[:, c * 256 : c * 256 + 256], groups) for c in range(blocks)]
    ok = jnp.ones((1, 256), f32)
    for c in range(blocks):
        e = jnp.exp2(scores(tturn[...], saug[:, c * 256 : c * 256 + 256]) - shifts[c])
        kept[:, c * 256 : c * 256 + 256] = e
        s = jnp.sum(jnp.sum(e.reshape(e.shape[0] // 8, 8, 256), 0), 0, keepdims=True)
        put(c, shifts[c] + jnp.log2(s), shifts[c])
        ok = jnp.minimum(ok, jnp.where(s < 2.0**40, 1.0, 0.0))

    @pl.when(jnp.min(ok) < 0.5)
    def _():
        exact_lse_blocks(tturn, saug, put, kept)

    for d in range(out.shape[0]):
        out[d, 16:17, :] = mass[...]


def second_body(part, kept, tops, tall, sall, out, taug, saug, sturn, held):
    held[...] = lse2(part[:, 0:16, :])
    factor = part[:, 16, :] * jnp.exp2(tops[...] - held[...])
    ok = jnp.ones((1, 128), f32)
    for k in range(tall.shape[0]):
        acc = jnp.zeros((128, 128), f32)
        for r in range(factor.shape[0]):
            acc = acc + kept[k * 128 : k * 128 + 128, r * 128 : r * 128 + 128] * factor[r : r + 1, :]
        s = jnp.sum(acc.T, 0, keepdims=True)
        line = jnp.log2(s) - first_bias(tall, k)
        for d in range(out.shape[0]):
            out[d, k : k + 1, :] = line
        ok = jnp.minimum(ok, jnp.where(s > 2.0**-50, 1.0, 0.0))

    @pl.when(jnp.min(ok) < 0.5)
    def _():
        fill_tgt(taug, None, tall, None)
        fill_src(saug, sturn, sall, lambda k: jnp.log2(part[k, 16:17, :]) - held[k : k + 1, :])
        exact_lse_blocks(sturn, taug, put_line(out))


def weigh(lhs, w):
    hi = w.astype(bf16)
    return scores(lhs, hi) + scores(lhs, (w - hi.astype(f32)).astype(bf16))


def third_body(part, kept, tops, tall, sall, out, pot, taug, tturn, saug, held, rows):
    held[...] = jnp.log2(tall[:, 17, :]) - lse2(part[...])
    count, blocks = taug.shape[1], saug.shape[1] // 256
    bias = jnp.concatenate([first_bias(tall, k) for k in range(tall.shape[0])], 0)
    ratio = held[...] - bias
    most = jnp.max(jnp.max(ratio, 0, keepdims=True), 1, keepdims=True)
    ratio = jnp.exp2(ratio - most)

    def fill_rows(factor):
        for k in range(tall.shape[0]):
            f = factor(k)
            cols = slice(k * 128, k * 128 + 128)
            rows[0:16, cols], rows[16:32, cols], rows[32:48, cols] = split3(tall[k, 0:16, :] * f)
            rows[48:64, cols] = bias_rows(f)

    def put(c, acc, top):
        s = acc[48:49, :] + acc[49:50, :] + acc[50:51, :]
        feats = (acc[0:16, :] + acc[16:32, :] + acc[32:48, :]) / s
        lse = top + jnp.log2(s)
        for h in range(2):
            out[2 * c + h, 0:16, :] = feats[:, h * 128 : h * 128 + 128]
            out[2 * c + h, 16:17, :] = lse[:, h * 128 : h * 128 + 128]
        return s

    fill_rows(lambda k: ratio[k : k + 1, :])
    ok = jnp.ones((1, 256), f32)
    for c in range(blocks):
        acc = jnp.zeros((64, 256), f32)
        for k in range(count // 1024):
            acc = acc + weigh(rows[:, k * 1024 : k * 1024 + 1024], kept[k * 1024 : k * 1024 + 1024, c * 256 : c * 256 + 256])
        top = jnp.concatenate([tops[2 * c : 2 * c + 1, :], tops[2 * c + 1 : 2 * c + 2, :]], 1)
        s = put(c, acc, top + most)
        ok = jnp.minimum(ok, jnp.where(s > 2.0**-50, 1.0, 0.0))

    @pl.when(jnp.min(ok) < 0.5)
    def _():
        fill_tgt(taug, tturn, tall, lambda k: held[k : k + 1, :])
        fill_src(saug, None, sall, None)
        fill_rows(lambda k: jnp.ones((1, 128), f32))

        @pl.loop(0, blocks)
        def _(c):
            rhs = saug[:, pl.ds(pl.multiple_of(c * 256, 256), 256)]
            top = full_top(tturn, rhs)

            def step(k, acc):
                at = pl.ds(pl.multiple_of(k * 256, 256), 256)
                return acc + weigh(rows[:, at], jnp.exp2(scores(tturn[at, :], rhs) - top))

            put(c, lax.fori_loop(0, count // 256, step, jnp.zeros((64, 256), f32)), top)


    masses = [jnp.sum(tall[:, row, :], 0, keepdims=True) for row in (18, 17)]
    for d in range(out.shape[0]):
        out[d, 17:18, :] = masses[0]
        out[d, 18:19, :] = masses[1]
    for z in range(pot.shape[0]):
        k = 2 * z + lax.axis_index("c")
        y = tall[pl.ds(k, 1), 0:16, :][0]
        pot[z : z + 1, :] = held[pl.ds(k, 1), :] / UNIT + jnp.sum(y * y, 0, keepdims=True)


def last_body(part, raw, sall, mass, src_pot, tgt_pot, bary):
    lses = part[:, 16, :]
    top = jnp.max(lses, 0, keepdims=True)
    w = jnp.exp2(lses - top)
    s = jnp.sum(w, 0, keepdims=True)
    acc = jnp.zeros((16, 128), f32)
    for k in range(part.shape[0]):
        acc = acc + part[k, 0:16, :] * w[k : k + 1, :]
    bary[...] = acc / s
    log_a, log_b = jnp.log2(total(part[:, 17, :])), jnp.log2(total(part[:, 18, :]))
    x = sall[0, 0:16, :]
    lse = top + jnp.log2(s)
    src_pot[...] = (jnp.log2(mass[...]) - lse + log_b - 2.0 * log_a) / UNIT + jnp.sum(x * x, 0, keepdims=True)
    tgt_pot[...] = raw[...] + (log_a - log_b) / UNIT


def call(body, outs, args, scratch=(), cost=None, where=pltpu.VMEM, limit=48):
    vmem = pl.BlockSpec(memory_space=pltpu.VMEM)
    return pl.pallas_call(
        body,
        out_shape=[jax.ShapeDtypeStruct(s, f32) for s in outs],
        in_specs=[pl.BlockSpec(memory_space=where)] * len(args),
        out_specs=[vmem] * len(outs),
        scratch_shapes=list(scratch),
        cost_estimate=cost,
        compiler_params=pltpu.CompilerParams(vmem_limit_bytes=limit << 20),
    )(*args)


def exchange(v, axes):
    return lax.all_to_all(v, axes, 0, 0, tiled=True)


def join_body(*refs):
    out, at = refs[-1], 0
    for ref in refs[:-1]:
        out[at : at + ref.shape[0]] = ref[...]
        at += ref.shape[0]


def join(parts, flops):
    shape = (sum(p.shape[0] for p in parts), *parts[0].shape[1:])
    return call(join_body, [shape], parts, cost=pl.CostEstimate(flops=flops, bytes_accessed=1000, transcendentals=0))[0]


def gather_rows(raw, own):
    for axis in ("x", "y"):
        moved = [lax.ppermute(raw, axis, [(i, (i + by) % 4) for i in range(4)]) for by in (1, 3, 2)]
        raw = own = join([own, *moved], 10**11) if axis == "x" else jnp.concatenate([own, *moved], 0)
    return own


def local(src_feat, tgt_feat, src_mass, tgt_mass, g_init):
    nt, ns = 16, 16
    taug, tturn = pltpu.VMEM((128, nt * 128), bf16), pltpu.VMEM((nt * 128, 128), bf16)
    saug, sturn = pltpu.VMEM((128, ns * 128), bf16), pltpu.VMEM((ns * 128, 128), bf16)
    ins = (src_feat, src_mass.reshape(1, 128), tgt_feat, tgt_mass.reshape(1, 128), g_init.reshape(8, 128))
    tmsg, own, smass = call(
        pack_body,
        [(nt, 19, 128), (1, 16, 128), (1, 128)],
        [pltpu.with_memory_space_constraint(v, pltpu.HBM) for v in ins],
        [pltpu.VMEM(s, f32) for s in ((16, 128), (1, 128), (8, 128))] + [pltpu.SemaphoreType.DMA((5,))],
        where=pltpu.HBM,
    )
    tall = exchange(tmsg, COLS)
    sall = gather_rows(src_feat.reshape(1, 16, 128), own)
    msg, kept, tops = call(
        first_body,
        [(ns, ns + 1, 128), (nt * 128, ns * 128), (ns, 128)],
        (tall, sall, smass),
        [taug, tturn, saug],
        limit=24,
    )
    first = exchange(msg, ROWS)
    (msg,) = call(
        second_body,
        [(nt, nt, 128)],
        (first, kept, tops, tall, sall),
        [taug, saug, sturn, pltpu.VMEM((ns, 128), f32)],
        limit=24,
    )
    second = exchange(msg, COLS)
    msg, raw = call(
        third_body,
        [(ns, 19, 128), (8, 128)],
        (second, kept, tops, tall, sall),
        [taug, tturn, saug, pltpu.VMEM((nt, 128), f32), pltpu.VMEM((64, nt * 128), bf16)],
        limit=24,
    )
    third = exchange(msg, ROWS)
    src_pot, tgt_pot, bary = call(last_body, [(1, 128), (8, 128), (16, 128)], (third, raw, sall, smass))
    return src_pot.reshape(128), tgt_pot.reshape(1024), bary


def solution(mesh):
    axes = ("z", "y", "x", "c")
    split = Mesh(mesh.devices.reshape(8, 4, 4, 2), axes)
    src, tgt = ("z", "y", "x", "c"), ("y", "x", "c", "z")
    return jax.shard_map(
        local,
        mesh=split,
        in_specs=(P(None, src), P(None, tgt), P(src), P(tgt), P(("y", "x", "c"))),
        out_specs=(P(src), P(("y", "x", "c")), P(None, src)),
        check_vma=False,
    )
```

```python
import functools

import jax
import jax.numpy as jnp
from jax import lax
from jax.experimental import pallas as pl
from jax.experimental.pallas import tpu as pltpu
from jax.sharding import Mesh, PartitionSpec as P

f32 = jnp.float32
bf16 = jnp.bfloat16
LOG2E = 1.4426950408889634
LN2 = 0.6931471805599453
epsilon = 0.5
UNIT = LOG2E / epsilon

T_ORDER = (0, 0, 1, 0, 1, 2)
S_ORDER = (0, 1, 0, 2, 1, 0)
COLS = ("z",)
ROWS = ("y", "x")


def split3(v):
    hi = v.astype(bf16)
    rest = v - hi.astype(f32)
    mid = rest.astype(bf16)
    return hi, mid, (rest - mid.astype(f32)).astype(bf16)


def bias_rows(row):
    hi, mid, lo = (jnp.broadcast_to(p.astype(f32), (16, 128)) for p in split3(row))
    r = lax.broadcasted_iota(jnp.int32, (16, 128), 0)
    return jnp.where(r == 0, hi, jnp.where(r == 1, mid, jnp.where(r == 2, lo, 0.0))).astype(bf16)


def put_feats(aug, k, feats, order):
    pieces = split3(feats)
    for at, which in enumerate(order):
        aug[at * 16 : at * 16 + 16, k * 128 : k * 128 + 128] = pieces[which]


class Targets:
    def __init__(self, mine, other):
        self.refs, self.count = (mine, other), 2 * mine.shape[0]

    def rows(self, k, first, last):
        c, z = divmod(k, self.count // 2)
        mine, other = (ref[z, first:last, :] for ref in self.refs)
        return jnp.where(lax.axis_index("c") == c, mine, other)

    def line(self, row):
        return jnp.concatenate([self.rows(k, row, row + 1) for k in range(self.count)], 0)


def fill_tgt(aug, turned, tall, bias):
    n = tall.count
    aug[112:128, :] = jnp.ones((16, n * 128), bf16)
    if bias is None:
        aug[96:112, :] = jnp.zeros((16, n * 128), bf16)
    for k in range(n):
        put_feats(aug, k, tall.rows(k, 0, 16), T_ORDER)
        if bias is not None:
            aug[96:112, k * 128 : k * 128 + 128] = bias_rows(bias(k))
            turned[k * 128 : k * 128 + 128, :] = aug[:, k * 128 : k * 128 + 128].T


def place(k):
    def pos(to, own):
        step = (to - own + 4) % 4
        return jnp.where(step == 0, 0, jnp.where(step == 1, 2, jnp.where(step == 2, 3, 1)))

    return pos(k // 4, lax.axis_index("y")) * 4 + pos(k % 4, lax.axis_index("x"))


def fill_src(aug, turned, sall, bias):
    n = sall.shape[0]
    aug[96:112, :] = jnp.ones((16, n * 128), bf16)
    if bias is None:
        aug[112:128, :] = jnp.zeros((16, n * 128), bf16)
    for k in range(n):
        put_feats(aug, k, sall[place(k), 0:16, :] * (2.0 * UNIT), S_ORDER)
        if bias is not None:
            aug[112:128, k * 128 : k * 128 + 128] = bias_rows(bias(k))
            turned[k * 128 : k * 128 + 128, :] = aug[:, k * 128 : k * 128 + 128].T


def scores(lhs, rhs):
    return lax.dot(lhs, rhs, preferred_element_type=f32)


def sample_top(lhs, rhs, groups):
    rows = lhs.shape[0] // groups
    some = jnp.concatenate([lhs[g * rows : g * rows + 16, :] for g in range(groups)], 0)
    return jnp.max(scores(some, rhs), 0, keepdims=True)


def full_top(lhs, rhs):
    def step(k, top):
        v = scores(lhs[pl.ds(pl.multiple_of(k * 256, 256), 256), :], rhs)
        return jnp.maximum(top, jnp.max(v, 0, keepdims=True))

    return lax.fori_loop(0, lhs.shape[0] // 256, step, jnp.full((1, rhs.shape[1]), -3e38, f32))


def exact_lse_blocks(lhs, aug, put, keep=None):
    @pl.loop(0, aug.shape[1] // 256)
    def _(c):
        cols = pl.ds(pl.multiple_of(c * 256, 256), 256)
        rhs = aug[:, cols]
        top = full_top(lhs, rhs)

        def step(k, s):
            rows = pl.ds(pl.multiple_of(k * 256, 256), 256)
            e = jnp.exp2(scores(lhs[rows, :], rhs) - top)
            if keep is not None:
                keep[rows, cols] = e
            return s + jnp.sum(e, 0, keepdims=True)

        s = lax.fori_loop(0, lhs.shape[0] // 256, step, jnp.zeros((1, 256), f32))
        put(c, top + jnp.log2(s), top)


def lse2(parts):
    top = jnp.max(parts, 0)
    return top + jnp.log2(jnp.sum(jnp.exp2(parts - top[None]), 0))


def total(rows):
    return jnp.sum(jnp.sum(rows, 0, keepdims=True), 1, keepdims=True)


def first_bias(tall, k):
    y = tall.rows(k, 0, 16)
    return UNIT * (tall.rows(k, 16, 17) - jnp.sum(y * y, 0, keepdims=True))


def pack_body(*refs):
    ins, (tmsg, src_feat, src_mass), held, sems = refs[:5], refs[5:8], refs[8:11], refs[11]
    tgt_feat, tgt_mass, g = held
    into = (src_feat.at[0], src_mass, tgt_feat, tgt_mass, g)
    copies = [pltpu.make_async_copy(a, b, sems.at[n]) for n, (a, b) in enumerate(zip(ins, into))]
    for copy in copies:
        copy.start()
    for copy in copies:
        copy.wait()
    g_own = g[pl.ds(lax.axis_index("z"), 1), :]
    for k in range(tmsg.shape[0]):
        tmsg[k, 0:16, :] = tgt_feat[...]
        tmsg[k, 16:17, :] = g_own
        tmsg[k, 17:18, :] = tgt_mass[...]
        tmsg[k, 18:19, :] = src_mass[...]


def put_line(out):
    def put(c, line, top=None):
        for d in range(out.shape[0]):
            out[d, pl.ds(2 * c, 1), :] = line[:, :128]
            out[d, pl.ds(2 * c + 1, 1), :] = line[:, 128:]

    return put


def first_body(mine, other, sall, mass, out, kept, tops, taug, tturn, saug):
    tall = Targets(mine, other)
    fill_tgt(taug, tturn, tall, lambda k: first_bias(tall, k))
    fill_src(saug, None, sall, None)

    def put(c, line, top):
        put_line(out)(c, line)
        tops[pl.ds(2 * c, 1), :] = top[:, :128]
        tops[pl.ds(2 * c + 1, 1), :] = top[:, 128:]

    blocks, groups = saug.shape[1] // 256, tturn.shape[0] // 256
    shifts = [sample_top(tturn, saug[:, c * 256 : c * 256 + 256], groups) for c in range(blocks)]
    ok = jnp.ones((1, 256), f32)
    for c in range(blocks):
        e = jnp.exp2(scores(tturn[...], saug[:, c * 256 : c * 256 + 256]) - shifts[c])
        kept[:, c * 256 : c * 256 + 256] = e
        s = jnp.sum(jnp.sum(e.reshape(e.shape[0] // 8, 8, 256), 0), 0, keepdims=True)
        put(c, shifts[c] + jnp.log2(s), shifts[c])
        ok = jnp.minimum(ok, jnp.where(s < 2.0**40, 1.0, 0.0))

    @pl.when(jnp.min(ok) < 0.5)
    def _():
        exact_lse_blocks(tturn, saug, put, kept)

    for d in range(out.shape[0]):
        out[d, 16:17, :] = mass[...]


def second_body(part, kept, tops, mine, other, sall, out, taug, saug, sturn, held):
    tall = Targets(mine, other)
    held[...] = lse2(part[:, 0:16, :])
    factor = part[:, 16, :] * jnp.exp2(tops[...] - held[...])
    ok = jnp.ones((1, 128), f32)
    for k in range(tall.count):
        acc = jnp.zeros((128, 128), f32)
        for r in range(factor.shape[0]):
            acc = acc + kept[k * 128 : k * 128 + 128, r * 128 : r * 128 + 128] * factor[r : r + 1, :]
        s = jnp.sum(acc.T, 0, keepdims=True)
        out[0, k : k + 1, :] = jnp.log2(s) - first_bias(tall, k)
        ok = jnp.minimum(ok, jnp.where(s > 2.0**-50, 1.0, 0.0))

    @pl.when(jnp.min(ok) < 0.5)
    def _():
        fill_tgt(taug, None, tall, None)
        fill_src(saug, sturn, sall, lambda k: jnp.log2(part[k, 16:17, :]) - held[k : k + 1, :])
        exact_lse_blocks(sturn, taug, put_line(out))


def pair_body(mine, other, out):
    both = lse2(jnp.concatenate([mine[...], other[...]], 0))
    for d in range(out.shape[0]):
        out[d] = both


def weigh(lhs, w):
    hi = w.astype(bf16)
    return scores(lhs, hi) + scores(lhs, (w - hi.astype(f32)).astype(bf16))


def third_body(part, kept, tops, mine, other, sall, out, pot, taug, tturn, saug, held, rows):
    tall = Targets(mine, other)
    held[...] = jnp.log2(tall.line(17)) - lse2(part[...])
    count, blocks = taug.shape[1], saug.shape[1] // 256
    bias = jnp.concatenate([first_bias(tall, k) for k in range(tall.count)], 0)
    ratio = held[...] - bias
    most = jnp.max(jnp.max(ratio, 0, keepdims=True), 1, keepdims=True)
    ratio = jnp.exp2(ratio - most)

    def fill_rows(factor):
        for k in range(tall.count):
            f = factor(k)
            cols = slice(k * 128, k * 128 + 128)
            rows[0:16, cols], rows[16:32, cols], rows[32:48, cols] = split3(tall.rows(k, 0, 16) * f)
            rows[48:64, cols] = bias_rows(f)

    def put(c, acc, top):
        s = acc[48:49, :] + acc[49:50, :] + acc[50:51, :]
        feats = (acc[0:16, :] + acc[16:32, :] + acc[32:48, :]) / s
        lse = top + jnp.log2(s)
        for h in range(2):
            out[2 * c + h, 0:16, :] = feats[:, h * 128 : h * 128 + 128]
            out[2 * c + h, 16:17, :] = lse[:, h * 128 : h * 128 + 128]
        return s

    fill_rows(lambda k: ratio[k : k + 1, :])
    ok = jnp.ones((1, 256), f32)
    for c in range(blocks):
        acc = jnp.zeros((64, 256), f32)
        for k in range(count // 1024):
            acc = acc + weigh(rows[:, k * 1024 : k * 1024 + 1024], kept[k * 1024 : k * 1024 + 1024, c * 256 : c * 256 + 256])
        top = jnp.concatenate([tops[2 * c : 2 * c + 1, :], tops[2 * c + 1 : 2 * c + 2, :]], 1)
        s = put(c, acc, top + most)
        ok = jnp.minimum(ok, jnp.where(s > 2.0**-50, 1.0, 0.0))

    @pl.when(jnp.min(ok) < 0.5)
    def _():
        fill_tgt(taug, tturn, tall, lambda k: held[k : k + 1, :])
        fill_src(saug, None, sall, None)
        fill_rows(lambda k: jnp.ones((1, 128), f32))

        @pl.loop(0, blocks)
        def _(c):
            rhs = saug[:, pl.ds(pl.multiple_of(c * 256, 256), 256)]
            top = full_top(tturn, rhs)

            def step(k, acc):
                at = pl.ds(pl.multiple_of(k * 256, 256), 256)
                return acc + weigh(rows[:, at], jnp.exp2(scores(tturn[at, :], rhs) - top))

            put(c, lax.fori_loop(0, count // 256, step, jnp.zeros((64, 256), f32)), top)


    masses = [jnp.sum(tall.line(row), 0, keepdims=True) for row in (18, 17)]
    for d in range(out.shape[0]):
        out[d, 17:18, :] = masses[0]
        out[d, 18:19, :] = masses[1]
    for z in range(pot.shape[0]):
        y = mine[z, 0:16, :]
        pot[z : z + 1, :] = held[pl.ds(lax.axis_index("c") * 8 + z, 1), :] / UNIT + jnp.sum(y * y, 0, keepdims=True)


def last_body(part, raw, sall, mass, src_pot, tgt_pot, bary):
    lses = part[:, 16, :]
    top = jnp.max(lses, 0, keepdims=True)
    w = jnp.exp2(lses - top)
    s = jnp.sum(w, 0, keepdims=True)
    acc = jnp.zeros((16, 128), f32)
    for k in range(part.shape[0]):
        acc = acc + part[k, 0:16, :] * w[k : k + 1, :]
    bary[...] = acc / s
    log_a, log_b = jnp.log2(total(part[:, 17, :])), jnp.log2(total(part[:, 18, :]))
    x = sall[0, 0:16, :]
    lse = top + jnp.log2(s)
    src_pot[...] = (jnp.log2(mass[...]) - lse + log_b - 2.0 * log_a) / UNIT + jnp.sum(x * x, 0, keepdims=True)
    tgt_pot[...] = raw[...] + (log_a - log_b) / UNIT


def call(body, outs, args, scratch=(), cost=None, where=pltpu.VMEM, limit=8):
    vmem = pl.BlockSpec(memory_space=pltpu.VMEM)
    return pl.pallas_call(
        body,
        out_shape=[jax.ShapeDtypeStruct(s, f32) for s in outs],
        in_specs=[pl.BlockSpec(memory_space=where)] * len(args),
        out_specs=[vmem] * len(outs),
        scratch_shapes=list(scratch),
        cost_estimate=cost,
        compiler_params=pltpu.CompilerParams(vmem_limit_bytes=limit << 20),
    )(*args)


def exchange(v, axes):
    return lax.all_to_all(v, axes, 0, 0, tiled=True)


def join_body(*refs):
    out, at = refs[-1], 0
    for ref in refs[:-1]:
        out[at : at + ref.shape[0]] = ref[...]
        at += ref.shape[0]


def join(parts, flops):
    shape = (sum(p.shape[0] for p in parts), *parts[0].shape[1:])
    return call(join_body, [shape], parts, cost=pl.CostEstimate(flops=flops, bytes_accessed=1000, transcendentals=0))[0]


def gather_rows(raw, own):
    for axis in ("x", "y"):
        moved = [lax.ppermute(raw, axis, [(i, (i + by) % 4) for i in range(4)]) for by in (1, 3, 2)]
        raw = own = join([own, *moved], 10**11) if axis == "x" else jnp.concatenate([own, *moved], 0)
    return own


def local(src_feat, tgt_feat, src_mass, tgt_mass, g_init):
    nt, ns = 16, 16
    taug, tturn = pltpu.VMEM((128, nt * 128), bf16), pltpu.VMEM((nt * 128, 128), bf16)
    saug, sturn = pltpu.VMEM((128, ns * 128), bf16), pltpu.VMEM((ns * 128, 128), bf16)
    ins = (src_feat, src_mass.reshape(1, 128), tgt_feat, tgt_mass.reshape(1, 128), g_init.reshape(8, 128))
    tmsg, own, smass = call(
        pack_body,
        [(8, 19, 128), (1, 16, 128), (1, 128)],
        [pltpu.with_memory_space_constraint(v, pltpu.HBM) for v in ins],
        [pltpu.VMEM(s, f32) for s in ((16, 128), (1, 128), (8, 128))] + [pltpu.SemaphoreType.DMA((5,))],
        where=pltpu.HBM,
    )
    mine = exchange(tmsg, COLS)
    other = lax.ppermute(mine, "c", [(0, 1), (1, 0)])
    sall = gather_rows(src_feat.reshape(1, 16, 128), own)
    msg, kept, tops = call(
        first_body,
        [(ns, ns + 1, 128), (nt * 128, ns * 128), (ns, 128)],
        (mine, other, sall, smass),
        [taug, tturn, saug],
        limit=24,
    )
    first = exchange(msg, ROWS)
    (msg,) = call(
        second_body,
        [(1, nt, 128)],
        (first, kept, tops, mine, other, sall),
        [taug, saug, sturn, pltpu.VMEM((ns, 128), f32)],
        limit=24,
    )
    (msg,) = call(pair_body, [(8, nt, 128)], (msg, lax.ppermute(msg, "c", [(0, 1), (1, 0)])))
    second = exchange(msg, COLS)
    msg, raw = call(
        third_body,
        [(ns, 19, 128), (8, 128)],
        (second, kept, tops, mine, other, sall),
        [taug, tturn, saug, pltpu.VMEM((nt, 128), f32), pltpu.VMEM((64, nt * 128), bf16)],
        limit=24,
    )
    third = exchange(msg, ROWS)
    src_pot, tgt_pot, bary = call(last_body, [(1, 128), (8, 128), (16, 128)], (third, raw, sall, smass))
    return src_pot.reshape(128), tgt_pot.reshape(1024), bary


def solution(mesh):
    axes = ("z", "y", "x", "c")
    split = Mesh(mesh.devices.reshape(8, 4, 4, 2), axes)
    src, tgt = ("z", "y", "x", "c"), ("y", "x", "c", "z")
    return jax.shard_map(
        local,
        mesh=split,
        in_specs=(P(None, src), P(None, tgt), P(src), P(tgt), P(("y", "x", "c"))),
        out_specs=(P(src), P(("y", "x", "c")), P(None, src)),
        check_vma=False,
    )
```

```python
import functools

import jax
import jax.numpy as jnp
from jax import lax
from jax.experimental import pallas as pl
from jax.experimental.pallas import tpu as pltpu
from jax.sharding import Mesh, PartitionSpec as P

f32 = jnp.float32
bf16 = jnp.bfloat16
LOG2E = 1.4426950408889634
LN2 = 0.6931471805599453
epsilon = 0.5
UNIT = LOG2E / epsilon

T_ORDER = (0, 0, 1, 0, 1, 2)
S_ORDER = (0, 1, 0, 2, 1, 0)
COLS = ("z",)
ROWS = ("y", "x")


def split3(v):
    hi = v.astype(bf16)
    rest = v - hi.astype(f32)
    mid = rest.astype(bf16)
    return hi, mid, (rest - mid.astype(f32)).astype(bf16)


def bias_rows(row):
    hi, mid, lo = (jnp.broadcast_to(p.astype(f32), (16, 128)) for p in split3(row))
    r = lax.broadcasted_iota(jnp.int32, (16, 128), 0)
    return jnp.where(r == 0, hi, jnp.where(r == 1, mid, jnp.where(r == 2, lo, 0.0))).astype(bf16)


def put_feats(aug, k, feats, order):
    pieces = split3(feats)
    for at, which in enumerate(order):
        aug[at * 16 : at * 16 + 16, k * 128 : k * 128 + 128] = pieces[which]


class Targets:
    def __init__(self, mine, other):
        self.refs, self.count = (mine, other), 2 * mine.shape[0]

    def rows(self, k, first, last):
        c, z = divmod(k, self.count // 2)
        mine, other = (ref[z, first:last, :] for ref in self.refs)
        return jnp.where(lax.axis_index("c") == c, mine, other)

    def line(self, row):
        return jnp.concatenate([self.rows(k, row, row + 1) for k in range(self.count)], 0)


def fill_tgt(aug, turned, tall, bias):
    n = tall.count
    aug[112:128, :] = jnp.ones((16, n * 128), bf16)
    if bias is None:
        aug[96:112, :] = jnp.zeros((16, n * 128), bf16)
    for k in range(n):
        put_feats(aug, k, tall.rows(k, 0, 16), T_ORDER)
        if bias is not None:
            aug[96:112, k * 128 : k * 128 + 128] = bias_rows(bias(k))
            turned[k * 128 : k * 128 + 128, :] = aug[:, k * 128 : k * 128 + 128].T


def ring_pos(to, own):
    step = (to - own + 4) % 4
    return jnp.where(step == 0, 0, jnp.where(step == 1, 2, jnp.where(step == 2, 3, 1)))


def place(k):
    return ring_pos(k // 4, lax.axis_index("y")) * 4 + (k % 4 ^ lax.axis_index("x"))


def fill_src(aug, turned, sall, bias):
    n = sall.shape[0]
    aug[96:112, :] = jnp.ones((16, n * 128), bf16)
    if bias is None:
        aug[112:128, :] = jnp.zeros((16, n * 128), bf16)
    for k in range(n):
        put_feats(aug, k, sall[place(k), 0:16, :] * (2.0 * UNIT), S_ORDER)
        if bias is not None:
            aug[112:128, k * 128 : k * 128 + 128] = bias_rows(bias(k))
            turned[k * 128 : k * 128 + 128, :] = aug[:, k * 128 : k * 128 + 128].T


def scores(lhs, rhs):
    return lax.dot(lhs, rhs, preferred_element_type=f32)


def sample_top(lhs, rhs, groups):
    rows = lhs.shape[0] // groups
    some = jnp.concatenate([lhs[g * rows : g * rows + 16, :] for g in range(groups)], 0)
    return jnp.max(scores(some, rhs), 0, keepdims=True)


def full_top(lhs, rhs):
    def step(k, top):
        v = scores(lhs[pl.ds(pl.multiple_of(k * 256, 256), 256), :], rhs)
        return jnp.maximum(top, jnp.max(v, 0, keepdims=True))

    return lax.fori_loop(0, lhs.shape[0] // 256, step, jnp.full((1, rhs.shape[1]), -3e38, f32))


def exact_lse_blocks(lhs, aug, put, keep=None):
    @pl.loop(0, aug.shape[1] // 256)
    def _(c):
        cols = pl.ds(pl.multiple_of(c * 256, 256), 256)
        rhs = aug[:, cols]
        top = full_top(lhs, rhs)

        def step(k, s):
            rows = pl.ds(pl.multiple_of(k * 256, 256), 256)
            e = jnp.exp2(scores(lhs[rows, :], rhs) - top)
            if keep is not None:
                keep[rows, cols] = e
            return s + jnp.sum(e, 0, keepdims=True)

        s = lax.fori_loop(0, lhs.shape[0] // 256, step, jnp.zeros((1, 256), f32))
        put(c, top + jnp.log2(s), top)


def lse2(parts):
    top = jnp.max(parts, 0)
    return top + jnp.log2(jnp.sum(jnp.exp2(parts - top[None]), 0))


def total(rows):
    return jnp.sum(jnp.sum(rows, 0, keepdims=True), 1, keepdims=True)


def first_bias(tall, k):
    y = tall.rows(k, 0, 16)
    return UNIT * (tall.rows(k, 16, 17) - jnp.sum(y * y, 0, keepdims=True))


def pack_body(*refs):
    ins, (tmsg, src_feat, src_mass), held, sems = refs[:5], refs[5:8], refs[8:11], refs[11]
    tgt_feat, tgt_mass, g = held
    into = (src_feat.at[0], src_mass, tgt_feat, tgt_mass, g)
    copies = [pltpu.make_async_copy(a, b, sems.at[n]) for n, (a, b) in enumerate(zip(ins, into))]
    for copy in copies:
        copy.start()
    for copy in copies:
        copy.wait()
    g_own = g[pl.ds(lax.axis_index("z"), 1), :]
    for k in range(tmsg.shape[0]):
        tmsg[k, 0:16, :] = tgt_feat[...]
        tmsg[k, 16:17, :] = g_own
        tmsg[k, 17:18, :] = tgt_mass[...]
        tmsg[k, 18:19, :] = src_mass[...]


def put_line(out):
    def put(c, line, top=None):
        for d in range(out.shape[0]):
            out[d, pl.ds(2 * c, 1), :] = line[:, :128]
            out[d, pl.ds(2 * c + 1, 1), :] = line[:, 128:]

    return put


def first_body(mine, other, sall, mass, out, kept, tops, taug, tturn, saug):
    tall = Targets(mine, other)
    fill_tgt(taug, tturn, tall, lambda k: first_bias(tall, k))
    fill_src(saug, None, sall, None)

    def put(c, line, top):
        put_line(out)(c, line)
        tops[pl.ds(2 * c, 1), :] = top[:, :128]
        tops[pl.ds(2 * c + 1, 1), :] = top[:, 128:]

    blocks, groups = saug.shape[1] // 256, tturn.shape[0] // 256
    shifts = [sample_top(tturn, saug[:, c * 256 : c * 256 + 256], groups) for c in range(blocks)]
    ok = jnp.ones((1, 256), f32)
    for c in range(blocks):
        e = jnp.exp2(scores(tturn[...], saug[:, c * 256 : c * 256 + 256]) - shifts[c])
        kept[:, c * 256 : c * 256 + 256] = e
        s = jnp.sum(jnp.sum(e.reshape(e.shape[0] // 8, 8, 256), 0), 0, keepdims=True)
        put(c, shifts[c] + jnp.log2(s), shifts[c])
        ok = jnp.minimum(ok, jnp.where(s < 2.0**40, 1.0, 0.0))

    @pl.when(jnp.min(ok) < 0.5)
    def _():
        exact_lse_blocks(tturn, saug, put, kept)

    for d in range(out.shape[0]):
        out[d, 16:17, :] = mass[...]


def second_body(part, kept, tops, mine, other, sall, out, taug, saug, sturn, held):
    tall = Targets(mine, other)
    held[...] = lse2(part[:, 0:16, :])
    factor = part[:, 16, :] * jnp.exp2(tops[...] - held[...])
    ok = jnp.ones((1, 128), f32)
    for k in range(tall.count):
        acc = jnp.zeros((128, 128), f32)
        for r in range(factor.shape[0]):
            acc = acc + kept[k * 128 : k * 128 + 128, r * 128 : r * 128 + 128] * factor[r : r + 1, :]
        s = jnp.sum(acc.T, 0, keepdims=True)
        out[0, k : k + 1, :] = jnp.log2(s) - first_bias(tall, k)
        ok = jnp.minimum(ok, jnp.where(s > 2.0**-50, 1.0, 0.0))

    @pl.when(jnp.min(ok) < 0.5)
    def _():
        fill_tgt(taug, None, tall, None)
        fill_src(saug, sturn, sall, lambda k: jnp.log2(part[k, 16:17, :]) - held[k : k + 1, :])
        exact_lse_blocks(sturn, taug, put_line(out))


def pair_body(mine, other, out):
    both = lse2(jnp.concatenate([mine[...], other[...]], 0))
    for d in range(out.shape[0]):
        out[d] = both


def weigh(lhs, w):
    hi = w.astype(bf16)
    return scores(lhs, hi) + scores(lhs, (w - hi.astype(f32)).astype(bf16))


def third_body(part, kept, tops, mine, other, sall, out, pot, taug, tturn, saug, held, rows):
    tall = Targets(mine, other)
    held[...] = jnp.log2(tall.line(17)) - lse2(part[...])
    count, blocks = taug.shape[1], saug.shape[1] // 256
    bias = jnp.concatenate([first_bias(tall, k) for k in range(tall.count)], 0)
    ratio = held[...] - bias
    most = jnp.max(jnp.max(ratio, 0, keepdims=True), 1, keepdims=True)
    ratio = jnp.exp2(ratio - most)

    def fill_rows(factor):
        for k in range(tall.count):
            f = factor(k)
            cols = slice(k * 128, k * 128 + 128)
            rows[0:16, cols], rows[16:32, cols], rows[32:48, cols] = split3(tall.rows(k, 0, 16) * f)
            rows[48:64, cols] = bias_rows(f)

    def put(c, acc, top):
        s = acc[48:49, :] + acc[49:50, :] + acc[50:51, :]
        feats = (acc[0:16, :] + acc[16:32, :] + acc[32:48, :]) / s
        lse = top + jnp.log2(s)
        for h in range(2):
            out[2 * c + h, 0:16, :] = feats[:, h * 128 : h * 128 + 128]
            out[2 * c + h, 16:17, :] = lse[:, h * 128 : h * 128 + 128]
        return s

    fill_rows(lambda k: ratio[k : k + 1, :])
    ok = jnp.ones((1, 256), f32)
    for c in range(blocks):
        acc = jnp.zeros((64, 256), f32)
        for k in range(count // 1024):
            acc = acc + weigh(rows[:, k * 1024 : k * 1024 + 1024], kept[k * 1024 : k * 1024 + 1024, c * 256 : c * 256 + 256])
        top = jnp.concatenate([tops[2 * c : 2 * c + 1, :], tops[2 * c + 1 : 2 * c + 2, :]], 1)
        s = put(c, acc, top + most)
        ok = jnp.minimum(ok, jnp.where(s > 2.0**-50, 1.0, 0.0))

    @pl.when(jnp.min(ok) < 0.5)
    def _():
        fill_tgt(taug, tturn, tall, lambda k: held[k : k + 1, :])
        fill_src(saug, None, sall, None)
        fill_rows(lambda k: jnp.ones((1, 128), f32))

        @pl.loop(0, blocks)
        def _(c):
            rhs = saug[:, pl.ds(pl.multiple_of(c * 256, 256), 256)]
            top = full_top(tturn, rhs)

            def step(k, acc):
                at = pl.ds(pl.multiple_of(k * 256, 256), 256)
                return acc + weigh(rows[:, at], jnp.exp2(scores(tturn[at, :], rhs) - top))

            put(c, lax.fori_loop(0, count // 256, step, jnp.zeros((64, 256), f32)), top)


    masses = [jnp.sum(tall.line(row), 0, keepdims=True) for row in (18, 17)]
    for d in range(out.shape[0]):
        out[d, 17:18, :] = masses[0]
        out[d, 18:19, :] = masses[1]
    for z in range(pot.shape[0]):
        y = mine[z, 0:16, :]
        pot[z : z + 1, :] = held[pl.ds(lax.axis_index("c") * 8 + z, 1), :] / UNIT + jnp.sum(y * y, 0, keepdims=True)


def last_body(part, raw, sall, mass, src_pot, tgt_pot, bary):
    lses = part[:, 16, :]
    top = jnp.max(lses, 0, keepdims=True)
    w = jnp.exp2(lses - top)
    s = jnp.sum(w, 0, keepdims=True)
    acc = jnp.zeros((16, 128), f32)
    for k in range(part.shape[0]):
        acc = acc + part[k, 0:16, :] * w[k : k + 1, :]
    bary[...] = acc / s
    log_a, log_b = jnp.log2(total(part[:, 17, :])), jnp.log2(total(part[:, 18, :]))
    x = sall[0, 0:16, :]
    lse = top + jnp.log2(s)
    src_pot[...] = (jnp.log2(mass[...]) - lse + log_b - 2.0 * log_a) / UNIT + jnp.sum(x * x, 0, keepdims=True)
    tgt_pot[...] = raw[...] + (log_a - log_b) / UNIT


def call(body, outs, args, scratch=(), cost=None, where=pltpu.VMEM, limit=8):
    vmem = pl.BlockSpec(memory_space=pltpu.VMEM)
    return pl.pallas_call(
        body,
        out_shape=[jax.ShapeDtypeStruct(s, f32) for s in outs],
        in_specs=[pl.BlockSpec(memory_space=where)] * len(args),
        out_specs=[vmem] * len(outs),
        scratch_shapes=list(scratch),
        cost_estimate=cost,
        compiler_params=pltpu.CompilerParams(vmem_limit_bytes=limit << 20),
    )(*args)


def exchange(v, axes):
    return lax.all_to_all(v, axes, 0, 0, tiled=True)


def join_body(*refs):
    out, at = refs[-1], 0
    for ref in refs[:-1]:
        out[at : at + ref.shape[0]] = ref[...]
        at += ref.shape[0]


def join(parts, flops):
    shape = (sum(p.shape[0] for p in parts), *parts[0].shape[1:])
    return call(join_body, [shape], parts, cost=pl.CostEstimate(flops=flops, bytes_accessed=1000, transcendentals=0))[0]


def gather_rows(raw, own):
    raw = own = join([own, lax.ppermute(raw, "x", [(i, i ^ 1) for i in range(4)])], 10**6)
    raw = own = join([own, lax.ppermute(raw, "x", [(i, i ^ 2) for i in range(4)])], 10**11)
    moved = [lax.ppermute(raw, "y", [(i, (i + by) % 4) for i in range(4)]) for by in (1, 3, 2)]
    raw = own = jnp.concatenate([own, *moved], 0)
    return own


def local(src_feat, tgt_feat, src_mass, tgt_mass, g_init):
    nt, ns = 16, 16
    taug, tturn = pltpu.VMEM((128, nt * 128), bf16), pltpu.VMEM((nt * 128, 128), bf16)
    saug, sturn = pltpu.VMEM((128, ns * 128), bf16), pltpu.VMEM((ns * 128, 128), bf16)
    ins = (src_feat, src_mass.reshape(1, 128), tgt_feat, tgt_mass.reshape(1, 128), g_init.reshape(8, 128))
    tmsg, own, smass = call(
        pack_body,
        [(8, 19, 128), (1, 16, 128), (1, 128)],
        [pltpu.with_memory_space_constraint(v, pltpu.HBM) for v in ins],
        [pltpu.VMEM(s, f32) for s in ((16, 128), (1, 128), (8, 128))] + [pltpu.SemaphoreType.DMA((5,))],
        where=pltpu.HBM,
    )
    mine = exchange(tmsg, COLS)
    other = lax.ppermute(mine, "c", [(0, 1), (1, 0)])
    sall = gather_rows(src_feat.reshape(1, 16, 128), own)
    msg, kept, tops = call(
        first_body,
        [(ns, ns + 1, 128), (nt * 128, ns * 128), (ns, 128)],
        (mine, other, sall, smass),
        [taug, tturn, saug],
        limit=24,
    )
    first = exchange(msg, ROWS)
    (msg,) = call(
        second_body,
        [(1, nt, 128)],
        (first, kept, tops, mine, other, sall),
        [taug, saug, sturn, pltpu.VMEM((ns, 128), f32)],
        limit=24,
    )
    (msg,) = call(pair_body, [(8, nt, 128)], (msg, lax.ppermute(msg, "c", [(0, 1), (1, 0)])))
    second = exchange(msg, COLS)
    msg, raw = call(
        third_body,
        [(ns, 19, 128), (8, 128)],
        (second, kept, tops, mine, other, sall),
        [taug, tturn, saug, pltpu.VMEM((nt, 128), f32), pltpu.VMEM((64, nt * 128), bf16)],
        limit=24,
    )
    third = exchange(msg, ROWS)
    src_pot, tgt_pot, bary = call(last_body, [(1, 128), (8, 128), (16, 128)], (third, raw, sall, smass))
    return src_pot.reshape(128), tgt_pot.reshape(1024), bary


def solution(mesh):
    axes = ("z", "y", "x", "c")
    split = Mesh(mesh.devices.reshape(8, 4, 4, 2), axes)
    src, tgt = ("z", "y", "x", "c"), ("y", "x", "c", "z")
    return jax.shard_map(
        local,
        mesh=split,
        in_specs=(P(None, src), P(None, tgt), P(src), P(tgt), P(("y", "x", "c"))),
        out_specs=(P(src), P(("y", "x", "c")), P(None, src)),
        check_vma=False,
    )
```

```python
import functools

import jax
import jax.numpy as jnp
from jax import lax
from jax.experimental import pallas as pl
from jax.experimental.pallas import tpu as pltpu
from jax.sharding import Mesh, PartitionSpec as P

f32 = jnp.float32
bf16 = jnp.bfloat16
LOG2E = 1.4426950408889634
LN2 = 0.6931471805599453
epsilon = 0.5
UNIT = LOG2E / epsilon

T_ORDER = (0, 0, 1, 0, 1, 2)
S_ORDER = (0, 1, 0, 2, 1, 0)
COLS = ("z",)
ROWS = ("y", "x")


def split3(v):
    hi = v.astype(bf16)
    rest = v - hi.astype(f32)
    mid = rest.astype(bf16)
    return hi, mid, (rest - mid.astype(f32)).astype(bf16)


def bias_rows(row):
    hi, mid, lo = (jnp.broadcast_to(p.astype(f32), (16, 128)) for p in split3(row))
    r = lax.broadcasted_iota(jnp.int32, (16, 128), 0)
    return jnp.where(r == 0, hi, jnp.where(r == 1, mid, jnp.where(r == 2, lo, 0.0))).astype(bf16)


def put_feats(aug, k, feats, order):
    pieces = split3(feats)
    for at, which in enumerate(order):
        aug[at * 16 : at * 16 + 16, k * 128 : k * 128 + 128] = pieces[which]


class Targets:
    def __init__(self, mine, other):
        self.refs, self.count = (mine, other), 2 * mine.shape[0]

    def rows(self, k, first, last):
        c, z = divmod(k, self.count // 2)
        mine, other = (ref[z, first:last, :] for ref in self.refs)
        return jnp.where(lax.axis_index("c") == c, mine, other)

    def line(self, row):
        return jnp.concatenate([self.rows(k, row, row + 1) for k in range(self.count)], 0)


def fill_tgt(aug, turned, tall, bias):
    n = tall.count
    aug[112:128, :] = jnp.ones((16, n * 128), bf16)
    if bias is None:
        aug[96:112, :] = jnp.zeros((16, n * 128), bf16)
    for k in range(n):
        put_feats(aug, k, tall.rows(k, 0, 16), T_ORDER)
        if bias is not None:
            aug[96:112, k * 128 : k * 128 + 128] = bias_rows(bias(k))
            turned[k * 128 : k * 128 + 128, :] = aug[:, k * 128 : k * 128 + 128].T


def ring_pos(to, own):
    step = (to - own + 4) % 4
    return jnp.where(step == 0, 0, jnp.where(step == 1, 2, jnp.where(step == 2, 3, 1)))


def place(k):
    return ring_pos(k // 4, lax.axis_index("y")) * 4 + (k % 4 ^ lax.axis_index("x"))


def fill_src(aug, turned, sall, bias):
    n = sall.shape[0]
    aug[96:112, :] = jnp.ones((16, n * 128), bf16)
    if bias is None:
        aug[112:128, :] = jnp.zeros((16, n * 128), bf16)
    for k in range(n):
        put_feats(aug, k, sall[place(k), 0:16, :] * (2.0 * UNIT), S_ORDER)
        if bias is not None:
            aug[112:128, k * 128 : k * 128 + 128] = bias_rows(bias(k))
            turned[k * 128 : k * 128 + 128, :] = aug[:, k * 128 : k * 128 + 128].T


def scores(lhs, rhs):
    return lax.dot(lhs, rhs, preferred_element_type=f32)


def sample_top(lhs, rhs, groups):
    rows = lhs.shape[0] // groups
    some = jnp.concatenate([lhs[g * rows : g * rows + 16, :] for g in range(groups)], 0)
    return jnp.max(scores(some, rhs), 0, keepdims=True)


def full_top(lhs, rhs):
    def step(k, top):
        v = scores(lhs[pl.ds(pl.multiple_of(k * 256, 256), 256), :], rhs)
        return jnp.maximum(top, jnp.max(v, 0, keepdims=True))

    return lax.fori_loop(0, lhs.shape[0] // 256, step, jnp.full((1, rhs.shape[1]), -3e38, f32))


def exact_lse_blocks(lhs, aug, put, keep=None):
    @pl.loop(0, aug.shape[1] // 256)
    def _(c):
        cols = pl.ds(pl.multiple_of(c * 256, 256), 256)
        rhs = aug[:, cols]
        top = full_top(lhs, rhs)

        def step(k, s):
            rows = pl.ds(pl.multiple_of(k * 256, 256), 256)
            e = jnp.exp2(scores(lhs[rows, :], rhs) - top)
            if keep is not None:
                keep[rows, cols] = e
            return s + jnp.sum(e, 0, keepdims=True)

        s = lax.fori_loop(0, lhs.shape[0] // 256, step, jnp.zeros((1, 256), f32))
        put(c, top + jnp.log2(s), top)


def lse2(parts):
    top = jnp.max(parts, 0)
    return top + jnp.log2(jnp.sum(jnp.exp2(parts - top[None]), 0))


def total(rows):
    return jnp.sum(jnp.sum(rows, 0, keepdims=True), 1, keepdims=True)


def first_bias(tall, k):
    y = tall.rows(k, 0, 16)
    return UNIT * (tall.rows(k, 16, 17) - jnp.sum(y * y, 0, keepdims=True))


def pack_body(*refs):
    ins, (tmsg, src_feat, src_mass), held, sems = refs[:5], refs[5:8], refs[8:11], refs[11]
    tgt_feat, tgt_mass, g = held
    into = (src_feat.at[0], src_mass, tgt_feat, tgt_mass, g)
    copies = [pltpu.make_async_copy(a, b, sems.at[n]) for n, (a, b) in enumerate(zip(ins, into))]
    for copy in copies:
        copy.start()
    for copy in copies:
        copy.wait()
    g_own = g[pl.ds(lax.axis_index("z"), 1), :]
    for k in range(tmsg.shape[0]):
        tmsg[k, 0:16, :] = tgt_feat[...]
        tmsg[k, 16:17, :] = g_own
        tmsg[k, 17:18, :] = tgt_mass[...]
        tmsg[k, 18:19, :] = src_mass[...]


def put_line(out):
    def put(c, line, top=None):
        for d in range(out.shape[0]):
            out[d, pl.ds(2 * c, 1), :] = line[:, :128]
            out[d, pl.ds(2 * c + 1, 1), :] = line[:, 128:]

    return put


def first_body(mine, other, sall, mass, out, kept, tops, taug, tturn, saug):
    tall = Targets(mine, other)
    fill_tgt(taug, tturn, tall, lambda k: first_bias(tall, k))
    fill_src(saug, None, sall, None)

    def put(c, line, top):
        put_line(out)(c, line)
        tops[pl.ds(2 * c, 1), :] = top[:, :128]
        tops[pl.ds(2 * c + 1, 1), :] = top[:, 128:]

    width, groups = 1024, tturn.shape[0] // 256
    blocks = [slice(at, at + width) for at in range(0, saug.shape[1], width)]
    shifts = [sample_top(tturn, saug[:, cols], groups) for cols in blocks]
    ok = jnp.ones((1, width), f32)
    for cols, shift in zip(blocks, shifts):
        e = jnp.exp2(scores(tturn[...], saug[:, cols]) - shift)
        kept[:, cols] = e
        s = jnp.sum(jnp.sum(e.reshape(e.shape[0] // 8, 8, width), 0), 0, keepdims=True)
        line = shift + jnp.log2(s)
        for at in range(0, width, 256):
            put((cols.start + at) // 256, line[:, at : at + 256], shift[:, at : at + 256])
        ok = jnp.minimum(ok, jnp.where(s < 2.0**40, 1.0, 0.0))

    @pl.when(jnp.min(ok) < 0.5)
    def _():
        exact_lse_blocks(tturn, saug, put, kept)

    for d in range(out.shape[0]):
        out[d, 16:17, :] = mass[...]


def second_body(part, kept, tops, mine, other, sall, out, taug, saug, sturn, held):
    tall = Targets(mine, other)
    held[...] = lse2(part[:, 0:16, :])
    factor = part[:, 16, :] * jnp.exp2(tops[...] - held[...])
    ok = jnp.ones((1, 128), f32)
    for k in range(tall.count):
        acc = jnp.zeros((128, 128), f32)
        for r in range(factor.shape[0]):
            acc = acc + kept[k * 128 : k * 128 + 128, r * 128 : r * 128 + 128] * factor[r : r + 1, :]
        s = jnp.sum(acc.T, 0, keepdims=True)
        out[0, k : k + 1, :] = jnp.log2(s) - first_bias(tall, k)
        ok = jnp.minimum(ok, jnp.where(s > 2.0**-50, 1.0, 0.0))

    @pl.when(jnp.min(ok) < 0.5)
    def _():
        fill_tgt(taug, None, tall, None)
        fill_src(saug, sturn, sall, lambda k: jnp.log2(part[k, 16:17, :]) - held[k : k + 1, :])
        exact_lse_blocks(sturn, taug, put_line(out))


def pair_body(mine, other, out):
    both = lse2(jnp.concatenate([mine[...], other[...]], 0))
    for d in range(out.shape[0]):
        out[d] = both


def weigh(lhs, w):
    hi = w.astype(bf16)
    return scores(lhs, hi) + scores(lhs, (w - hi.astype(f32)).astype(bf16))


def third_body(part, kept, tops, mine, other, sall, out, pot, taug, tturn, saug, held, rows):
    tall = Targets(mine, other)
    held[...] = jnp.log2(tall.line(17)) - lse2(part[...])
    count, blocks = taug.shape[1], saug.shape[1] // 256
    bias = jnp.concatenate([first_bias(tall, k) for k in range(tall.count)], 0)
    ratio = held[...] - bias
    most = jnp.max(jnp.max(ratio, 0, keepdims=True), 1, keepdims=True)
    ratio = jnp.exp2(ratio - most)

    def fill_rows(factor):
        for k in range(tall.count):
            f = factor(k)
            cols = slice(k * 128, k * 128 + 128)
            rows[0:16, cols], rows[16:32, cols], rows[32:48, cols] = split3(tall.rows(k, 0, 16) * f)
            rows[48:64, cols] = bias_rows(f)

    def put(c, acc, top):
        s = acc[48:49, :] + acc[49:50, :] + acc[50:51, :]
        feats = (acc[0:16, :] + acc[16:32, :] + acc[32:48, :]) / s
        lse = top + jnp.log2(s)
        for h in range(2):
            out[2 * c + h, 0:16, :] = feats[:, h * 128 : h * 128 + 128]
            out[2 * c + h, 16:17, :] = lse[:, h * 128 : h * 128 + 128]
        return s

    fill_rows(lambda k: ratio[k : k + 1, :])
    ok = jnp.ones((1, 256), f32)
    for c in range(blocks):
        acc = jnp.zeros((64, 256), f32)
        for k in range(count // 1024):
            acc = acc + weigh(rows[:, k * 1024 : k * 1024 + 1024], kept[k * 1024 : k * 1024 + 1024, c * 256 : c * 256 + 256])
        top = jnp.concatenate([tops[2 * c : 2 * c + 1, :], tops[2 * c + 1 : 2 * c + 2, :]], 1)
        s = put(c, acc, top + most)
        ok = jnp.minimum(ok, jnp.where(s > 2.0**-50, 1.0, 0.0))

    @pl.when(jnp.min(ok) < 0.5)
    def _():
        fill_tgt(taug, tturn, tall, lambda k: held[k : k + 1, :])
        fill_src(saug, None, sall, None)
        fill_rows(lambda k: jnp.ones((1, 128), f32))

        @pl.loop(0, blocks)
        def _(c):
            rhs = saug[:, pl.ds(pl.multiple_of(c * 256, 256), 256)]
            top = full_top(tturn, rhs)

            def step(k, acc):
                at = pl.ds(pl.multiple_of(k * 256, 256), 256)
                return acc + weigh(rows[:, at], jnp.exp2(scores(tturn[at, :], rhs) - top))

            put(c, lax.fori_loop(0, count // 256, step, jnp.zeros((64, 256), f32)), top)


    masses = [jnp.sum(tall.line(row), 0, keepdims=True) for row in (18, 17)]
    for d in range(out.shape[0]):
        out[d, 17:18, :] = masses[0]
        out[d, 18:19, :] = masses[1]
    for z in range(pot.shape[0]):
        y = mine[z, 0:16, :]
        pot[z : z + 1, :] = held[pl.ds(lax.axis_index("c") * 8 + z, 1), :] / UNIT + jnp.sum(y * y, 0, keepdims=True)


def last_body(part, raw, sall, mass, src_pot, tgt_pot, bary):
    lses = part[:, 16, :]
    top = jnp.max(lses, 0, keepdims=True)
    w = jnp.exp2(lses - top)
    s = jnp.sum(w, 0, keepdims=True)
    acc = jnp.zeros((16, 128), f32)
    for k in range(part.shape[0]):
        acc = acc + part[k, 0:16, :] * w[k : k + 1, :]
    bary[...] = acc / s
    log_a, log_b = jnp.log2(total(part[:, 17, :])), jnp.log2(total(part[:, 18, :]))
    x = sall[0, 0:16, :]
    lse = top + jnp.log2(s)
    src_pot[...] = (jnp.log2(mass[...]) - lse + log_b - 2.0 * log_a) / UNIT + jnp.sum(x * x, 0, keepdims=True)
    tgt_pot[...] = raw[...] + (log_a - log_b) / UNIT


def call(body, outs, args, scratch=(), cost=None, where=pltpu.VMEM, limit=8):
    vmem = pl.BlockSpec(memory_space=pltpu.VMEM)
    return pl.pallas_call(
        body,
        out_shape=[jax.ShapeDtypeStruct(s, f32) for s in outs],
        in_specs=[pl.BlockSpec(memory_space=where)] * len(args),
        out_specs=[vmem] * len(outs),
        scratch_shapes=list(scratch),
        cost_estimate=cost,
        compiler_params=pltpu.CompilerParams(vmem_limit_bytes=limit << 20),
    )(*args)


def exchange(v, axes):
    return lax.all_to_all(v, axes, 0, 0, tiled=True)


def join_body(*refs):
    out, at = refs[-1], 0
    for ref in refs[:-1]:
        out[at : at + ref.shape[0]] = ref[...]
        at += ref.shape[0]


def join(parts, flops):
    shape = (sum(p.shape[0] for p in parts), *parts[0].shape[1:])
    return call(join_body, [shape], parts, cost=pl.CostEstimate(flops=flops, bytes_accessed=1000, transcendentals=0))[0]


def gather_rows(raw, own):
    raw = own = join([own, lax.ppermute(raw, "x", [(i, i ^ 1) for i in range(4)])], 10**6)
    raw = own = join([own, lax.ppermute(raw, "x", [(i, i ^ 2) for i in range(4)])], 10**11)
    moved = [lax.ppermute(raw, "y", [(i, (i + by) % 4) for i in range(4)]) for by in (1, 3, 2)]
    raw = own = jnp.concatenate([own, *moved], 0)
    return own


def local(src_feat, tgt_feat, src_mass, tgt_mass, g_init):
    nt, ns = 16, 16
    taug, tturn = pltpu.VMEM((128, nt * 128), bf16), pltpu.VMEM((nt * 128, 128), bf16)
    saug, sturn = pltpu.VMEM((128, ns * 128), bf16), pltpu.VMEM((ns * 128, 128), bf16)
    ins = (src_feat, src_mass.reshape(1, 128), tgt_feat, tgt_mass.reshape(1, 128), g_init.reshape(8, 128))
    tmsg, own, smass = call(
        pack_body,
        [(8, 19, 128), (1, 16, 128), (1, 128)],
        [pltpu.with_memory_space_constraint(v, pltpu.HBM) for v in ins],
        [pltpu.VMEM(s, f32) for s in ((16, 128), (1, 128), (8, 128))] + [pltpu.SemaphoreType.DMA((5,))],
        where=pltpu.HBM,
    )
    mine = exchange(tmsg, COLS)
    other = lax.ppermute(mine, "c", [(0, 1), (1, 0)])
    sall = gather_rows(src_feat.reshape(1, 16, 128), own)
    msg, kept, tops = call(
        first_body,
        [(ns, ns + 1, 128), (nt * 128, ns * 128), (ns, 128)],
        (mine, other, sall, smass),
        [taug, tturn, saug],
        limit=24,
    )
    first = exchange(msg, ROWS)
    (msg,) = call(
        second_body,
        [(1, nt, 128)],
        (first, kept, tops, mine, other, sall),
        [taug, saug, sturn, pltpu.VMEM((ns, 128), f32)],
        limit=24,
    )
    (msg,) = call(pair_body, [(8, nt, 128)], (msg, lax.ppermute(msg, "c", [(0, 1), (1, 0)])))
    second = exchange(msg, COLS)
    msg, raw = call(
        third_body,
        [(ns, 19, 128), (8, 128)],
        (second, kept, tops, mine, other, sall),
        [taug, tturn, saug, pltpu.VMEM((nt, 128), f32), pltpu.VMEM((64, nt * 128), bf16)],
        limit=24,
    )
    third = exchange(msg, ROWS)
    src_pot, tgt_pot, bary = call(last_body, [(1, 128), (8, 128), (16, 128)], (third, raw, sall, smass))
    return src_pot.reshape(128), tgt_pot.reshape(1024), bary


def solution(mesh):
    axes = ("z", "y", "x", "c")
    split = Mesh(mesh.devices.reshape(8, 4, 4, 2), axes)
    src, tgt = ("z", "y", "x", "c"), ("y", "x", "c", "z")
    return jax.shard_map(
        local,
        mesh=split,
        in_specs=(P(None, src), P(None, tgt), P(src), P(tgt), P(("y", "x", "c"))),
        out_specs=(P(src), P(("y", "x", "c")), P(None, src)),
        check_vma=False,
    )
```
